256 devices in a mesh: blk: 64 (over z, x, core), rep: 4 (over y).
Axes of the slice: x: 4, y: 4, z: 8, core: 2. Of those that a mesh axis runs over, the one named last changes fastest.
Arguments:
- embeddings: float32 [12288, 256], P('blk'), may hold values from -3 to 3
- partner: int32 [12288], P('blk'), may hold values from 0 to 12287, as said below
Outputs:
- view_loss: float32 [12288], P('blk')
- grad: float32 [12288, 256], P('blk')
The draws below stay inside these ranges and needn't reach their ends.
Inputs may be any that keep to these rules, and one draw needn't show every extreme that they name: A view's partner is another view of the same block of 192 views, and the partner's partner is the view itself.
All inputs are finite; a program needn't handle non-finite values.
Results may differ from the reference program's by a relative error of at most 0.0003.
Values sent between devices are 32-bit elements; how exact they have to be, the bound alone decides.
A program may use at most 128 MiB of HBM per device.

```python
import jax
import jax.numpy as jnp
from jax import lax

P_SIZE = 256
ROWS = 192
BLOCKS = 64
VIEWS = 12288


def draw_embeddings(key, part):
    key = jax.random.fold_in(key, 11)
    key_centers, key_labels, key_noise, key_scales = jax.random.split(key, 4)
    centers = jax.random.truncated_normal(key_centers, -4.0, 4.0, (16, P_SIZE), jnp.float32)
    labels = jax.random.randint(key_labels, (VIEWS,), 0, 16)
    noise = jax.random.truncated_normal(key_noise, -4.0, 4.0, (VIEWS, P_SIZE), jnp.float32)
    scales = jnp.exp(jax.random.uniform(key_scales, (VIEWS, 1), jnp.float32, -1.2, 1.2))
    return ((centers[labels] + noise) * scales / 16.0).astype(jnp.float32)


def draw_partner(key, part):
    key = jax.random.fold_in(key, 12)
    keys = jax.random.split(key, BLOCKS)
    perms = jax.vmap(lambda k: jax.random.permutation(k, ROWS))(keys).astype(jnp.int32)
    swapped = perms.reshape(BLOCKS, ROWS // 2, 2)[:, :, ::-1].reshape(BLOCKS, ROWS)
    empty = jnp.zeros((BLOCKS, ROWS), jnp.int32)
    local = jax.vmap(lambda base, order, mates: base.at[order].set(mates))(empty, perms, swapped)
    offsets = (jnp.arange(BLOCKS, dtype=jnp.int32) * ROWS)[:, None]
    return (local + offsets).reshape(-1).astype(jnp.int32)


def setup_inputs(seed: int = 0) -> dict:
    arg_keys = jax.random.split(jax.random.key(seed), 3)
    return {
        "embeddings": draw_embeddings(jax.random.fold_in(arg_keys[2], 71), 0),
        "partner": draw_partner(jax.random.fold_in(arg_keys[2], 71), 0),
    }


INV_TEMP = 10.0

def reference(embeddings, partner):
    views = embeddings.shape[0]
    blocks = views // ROWS
    norms = jnp.sqrt(lax.optimization_barrier(jnp.sum(embeddings * embeddings, axis=1, keepdims=True)) + 1e-12)
    unit = embeddings / norms
    column_ids = jnp.arange(views, dtype=jnp.int32)

    def block_scores(index):
        rows_unit = lax.dynamic_slice_in_dim(unit, (index * ROWS).astype(jnp.int32), ROWS, 0)
        scores = jnp.dot(rows_unit, unit.T, precision=lax.Precision.HIGHEST, preferred_element_type=jnp.float32) * INV_TEMP
        row_ids = index * ROWS + jnp.arange(ROWS, dtype=jnp.int32)
        keep = (row_ids[:, None] != column_ids[None, :]).astype(jnp.float32)
        return (scores, keep)

    def forward(index):
        scores, keep = block_scores(index)
        return jnp.log(lax.optimization_barrier(jnp.sum(jnp.exp(scores - INV_TEMP) * keep, axis=1))) + INV_TEMP
    lse = lax.map(forward, jnp.arange(blocks, dtype=jnp.int32)).reshape(views)

    def backward(index):
        scores, keep = block_scores(index)
        own = lax.dynamic_slice_in_dim(lse, (index * ROWS).astype(jnp.int32), ROWS, 0)
        both = (jnp.exp(scores - own[:, None]) + jnp.exp(scores - lse[None, :])) * keep
        return jnp.dot(both, unit, precision=lax.Precision.HIGHEST, preferred_element_type=jnp.float32)
    pull = lax.map(backward, jnp.arange(blocks, dtype=jnp.int32)).reshape(views, -1)
    mates = unit[partner]
    view_loss = lse - INV_TEMP * lax.optimization_barrier(jnp.sum(unit * mates, axis=1))
    grad_unit = INV_TEMP * (pull - 2.0 * mates)
    grad = (grad_unit - unit * lax.optimization_barrier(jnp.sum(unit * grad_unit, axis=1, keepdims=True))) / norms
    return (view_loss, grad)
```

```python
import jax
import jax.numpy as jnp
from jax import lax
from jax.experimental import pallas as pl
from jax.experimental.pallas import tpu as pltpu
from jax.sharding import PartitionSpec as P

MESH = pl.DeviceIdType.MESH
F32 = jnp.float32
BF16 = jnp.bfloat16
HIGHEST = lax.Precision.HIGHEST
INV_TEMP = 10.0
ROWS = 192
WIDTH = 256
XS, YS, ZS, CORES = 4, 4, 8, 2
CHUNKS = 2
CHUNK = ROWS // CHUNKS
SHARE = ROWS // YS


def dot_nn(a, b, precision=None):
    return lax.dot_general(
        a, b, (((1,), (0,)), ((), ())), precision=precision, preferred_element_type=F32
    )


def dot_nt(a, b, precision=None):
    return lax.dot_general(
        a, b, (((1,), (1,)), ((), ())), precision=precision, preferred_element_type=F32
    )


def split(value):
    high = value.astype(BF16)
    return high, (value - high.astype(F32)).astype(BF16)


def kernel(
    emb_ref,
    partner_ref,
    loss_ref,
    grad_ref,
    ui,
    ui_hi,
    ui_lo,
    norms,
    mates,
    uj,
    uj_hi,
    uj_lo,
    weights,
    acc,
    sums,
    inverse,
    inverse_rows,
    inverse_cols,
    pull_out,
    pull_in,
    pull_own,
    shares,
    gather_send,
    gather_recv,
    own_send,
    sums_send,
    sums_recv,
    inv_send,
    inv_recv,
    sib_send,
    sib_recv,
    share_send,
    share_recv,
    grad_send,
    grad_recv,
):
    blk = lax.axis_index("blk")
    y = lax.axis_index("rep")
    core = lax.rem(blk, CORES)
    x = lax.rem(lax.div(blk, CORES), XS)
    z = lax.div(blk, CORES * XS)

    def device(dx=0, dy=0, dz=0, dc=0):
        there = lax.rem(z + (dz % ZS), ZS) * XS + lax.rem(x + (dx % XS), XS)
        return (there * CORES + lax.rem(core + dc, CORES), lax.rem(y + (dy % YS), YS))

    is_a = core == 0
    is_b = core == 1
    offset = lax.rem(z + ZS - y, 4)
    a_source = jnp.logical_and(is_a, offset == 0)
    b_source = jnp.logical_and(is_b, x == y)
    is_source = jnp.logical_or(a_source, b_source)
    own_rows = pl.ds(pl.multiple_of(core * ROWS, ROWS), ROWS)
    sib_rows = pl.ds(pl.multiple_of((1 - core) * ROWS, ROWS), ROWS)

    group = [(dy, dc) for dc in range(CORES) for dy in range(YS) if (dy, dc) != (0, 0)]
    near = [device(dy=dy, dc=dc) for dy, dc in group]
    near += [device(dx=d) for d in (1, 2, 3)] + [device(dz=d) for d in (1, 7)]
    barrier = pltpu.get_barrier_semaphore()
    for peer in near:
        pl.semaphore_signal(barrier, inc=1, device_id=peer, device_id_type=MESH)

    emb = emb_ref[...]
    norm = jnp.sqrt(jnp.sum(emb * emb, axis=1, keepdims=True) + 1e-12)
    unit = emb / norm
    norms[...] = norm
    ui[own_rows, :] = unit

    @pl.when(is_source)
    def _():
        uj[0] = unit

    pl.semaphore_wait(barrier, len(near))

    sent = []

    def send(cond, src, dst, send_sem, recv_sem, peer):
        copy = pltpu.make_async_remote_copy(
            src_ref=src,
            dst_ref=dst,
            send_sem=send_sem,
            recv_sem=recv_sem,
            device_id=peer,
            device_id_type=MESH,
        )
        if cond is None:
            copy.start()
        else:
            pl.when(cond)(copy.start)
        sent.append((cond, copy))

    def arrived(dst, recv_sem):
        pltpu.make_async_remote_copy(
            src_ref=dst,
            dst_ref=dst,
            send_sem=recv_sem,
            recv_sem=recv_sem,
            device_id=device(dc=1),
            device_id_type=MESH,
        ).wait_recv()

    def part(slot, h):
        return uj.at[slot, pl.ds(h * CHUNK, CHUNK)]

    def forward(cond, slot, to_slot, h, lane, peer):
        send(
            cond,
            part(slot, h),
            part(to_slot, h),
            gather_send.at[slot, h, lane],
            gather_recv.at[to_slot, h],
            peer,
        )

    def await_part(cond, slot, h):
        def wait():
            arrived(part(slot, h), gather_recv.at[slot, h])

        pl.when(cond)(wait)

    both = range(CHUNKS)
    last_half = CHUNKS // 2

    send(None, ui.at[own_rows], ui.at[own_rows], own_send, sib_recv.at[1], device(dc=1))

    def x_spread(cond, slot, h):
        forward(cond, slot, slot + 1, h, 2, device(dx=1))
        forward(cond, slot, slot + 2, h, 3, device(dx=-1))

    a_other = jnp.logical_and(is_a, offset != 0)
    b_other = jnp.logical_and(is_b, x != y)
    near_up = jnp.logical_and(is_a, jnp.logical_or(offset == 1, offset == 2))
    near_down = jnp.logical_and(is_a, offset == 3)
    near_to = jnp.where(offset >= 2, 3, 0)
    for h in both:
        forward(a_source, 0, 0, h, 0, device(dz=1))
        forward(a_source, 0, 0, h, 1, device(dz=-1))
        x_spread(a_source, 0, h)
        forward(b_source, 0, 0, h, 2, device(dx=2))
        forward(b_source, 0, 0, h, 3, device(dx=1))
        forward(b_source, 0, 0, h, 4, device(dx=-1))
        forward(b_source, 0, 1, h, 0, device(dz=1))
        forward(b_source, 0, 2, h, 1, device(dz=-1))
    for h in both:
        await_part(jnp.logical_not(is_source), 0, h)
        forward(near_up, 0, near_to, h, 0, device(dz=1))
        forward(near_down, 0, near_to, h, 1, device(dz=-1))
        x_spread(a_other, 0, h)
        forward(b_other, 0, 1, h, 0, device(dz=1))
        forward(b_other, 0, 2, h, 1, device(dz=-1))

    def far_column(cond):
        far_up = jnp.logical_and(cond, offset == 3)
        far_down = jnp.logical_and(cond, jnp.logical_or(offset == 1, offset == 2))
        for h in both:
            await_part(cond, 3, h)
            if h < last_half:
                forward(far_up, 3, 3, h, 0, device(dz=1))
                forward(
                    jnp.logical_and(cond, offset == 2), 3, 3, h, 1, device(dz=-1)
                )
            else:
                forward(far_down, 3, 3, h, 1, device(dz=-1))
            x_spread(cond, 3, h)

    far_column(jnp.logical_and(is_a, offset == 2))

    def a_pair(left, right, to):
        for h in both:
            await_part(is_a, left, h)
            if h < last_half:
                forward(is_a, left, to, h, 2, device(dx=1))
            await_part(is_a, right, h)
            if h >= last_half:
                forward(is_a, right, to, h, 3, device(dx=-1))

    def b_pair(up, down):
        for h in both:
            await_part(is_b, up, h)
            if up < 5:
                forward(is_b, up, up + 2, h, 0, device(dz=1))
            elif h < last_half:
                forward(is_b, up, 7, h, 0, device(dz=1))
            await_part(is_b, down, h)
            if down < 6:
                forward(is_b, down, down + 2, h, 1, device(dz=-1))
            elif h >= last_half:
                forward(is_b, down, 7, h, 1, device(dz=-1))

    def scores(slot):
        high, low = split(uj[slot])
        uj_hi[slot] = high
        uj_lo[slot] = low
        left, left_low = ui_hi[...], ui_lo[...]
        score = dot_nt(left, high) + dot_nt(left_low, high) + dot_nt(left, low)
        weight = jnp.exp(score * INV_TEMP - INV_TEMP)
        if slot == 0:
            row = lax.broadcasted_iota(jnp.int32, weight.shape, 0)
            col = lax.broadcasted_iota(jnp.int32, weight.shape, 1)
            start = jnp.where(is_source, core * ROWS, 2 * CORES * ROWS)
            weight = jnp.where(row == col + start, 0.0, weight)
            acc[...] = weight
        else:
            acc[...] += weight
        weights[slot] = weight

    arrived(ui.at[sib_rows], sib_recv.at[1])
    high, low = split(ui[...])
    ui_hi[...] = high
    ui_lo[...] = low
    scores(0)
    a_pair(1, 2, 6)
    b_pair(1, 2)
    scores(1)
    scores(2)
    far_column(jnp.logical_and(is_a, offset != 2))
    b_pair(3, 4)
    scores(3)
    a_pair(4, 5, 7)
    scores(4)
    b_pair(5, 6)
    scores(5)
    for h in both:
        await_part(is_a, 6, h)
    scores(6)
    for h in both:
        await_part(is_a, 7, h)
        await_part(is_b, 7, h)
    scores(7)

    mine = y * CORES + core
    ones = jnp.ones((8, ROWS), F32)
    for c in range(CORES):
        sums[mine, c] = dot_nt(ones, acc[c * ROWS : (c + 1) * ROWS, :], HIGHEST)[0:1]
    for i, (dy, dc) in enumerate(group):
        send(
            None,
            sums.at[mine],
            sums.at[mine],
            sums_send.at[i],
            sums_recv.at[mine],
            device(dy=dy, dc=dc),
        )
    unit = ui[own_rows, :]
    node = lax.broadcasted_iota(jnp.int32, (ROWS, ROWS), 0)
    pairing = (node == partner_ref[...]).astype(F32)
    mate = dot_nn(pairing, unit, HIGHEST)
    mates[...] = mate
    pair_score = dot_nt(jnp.ones((8, WIDTH), F32), unit * mate, HIGHEST)[0:1]
    for dy, dc in group:
        other = lax.rem(y + dy, YS) * CORES + lax.rem(core + dc, CORES)
        arrived(sums.at[other], sums_recv.at[other])
    total = sums[0]
    for i in range(1, YS * CORES):
        total = total + sums[i]
    inverse[...] = 1.0 / total

    plane = jnp.where(is_a, lax.rem(z, 4), x)
    shift = lax.rem(2 + y + YS - plane, YS)
    column = jnp.where(shift == 2, 3, jnp.where(shift == 3, 2, shift))
    for dz in range(ZS):
        far_slot = jnp.where(column == 3, 7, column + 3)
        near_slot = jnp.where(column == 3, 6, column)
        a_slot = near_slot if dz in (0, 1, 2, 7) else far_slot
        b_slot = (0, 1, 3, 5, 7, 6, 4, 2)[dz]
        slot = jnp.where(is_a, a_slot, b_slot)
        there = lax.rem(z + dz, ZS) * XS + lax.rem(x + shift, XS)
        send(
            None,
            inverse.at[core],
            inverse_cols.at[slot],
            inv_send.at[dz],
            inv_recv.at[slot],
            (there * CORES + core, plane),
        )
    loss_ref[...] = jnp.log(jnp.where(is_a, total[0], total[1])) + INV_TEMP - INV_TEMP * pair_score
    same = lax.broadcasted_iota(jnp.int32, (ROWS, ROWS), 1) == node
    for c in range(CORES):
        column_sum = jnp.sum(jnp.where(same, inverse[c], 0.0), axis=1, keepdims=True)
        inverse_rows[c * ROWS : (c + 1) * ROWS, :] = jnp.broadcast_to(column_sum, (ROWS, ROWS))
    for slot in range(8):
        arrived(inverse_cols.at[slot], inv_recv.at[slot])

    def pulls(rows):
        total = jnp.zeros((ROWS, WIDTH), F32)
        for slot in range(8):
            both = weights[slot, rows, :] * (inverse_rows[rows, :] + inverse_cols[slot])
            high, low = split(both)
            total = total + dot_nn(high, uj_hi[slot])
            total = total + dot_nn(low, uj_hi[slot])
            total = total + dot_nn(high, uj_lo[slot])
        return total

    pull_out[...] = pulls(sib_rows)
    send(None, pull_out, pull_in, sib_send, sib_recv.at[0], device(dc=1))
    own = pulls(own_rows)
    arrived(pull_in, sib_recv.at[0])
    pull_own[...] = own + pull_in[...]
    for dy in range(1, YS):
        rows = pl.ds(pl.multiple_of(lax.rem(y + dy, YS) * SHARE, SHARE), SHARE)
        send(
            None,
            pull_own.at[rows],
            shares.at[dy - 1],
            share_send.at[dy - 1],
            share_recv.at[dy - 1],
            device(dy=dy),
        )
    for dy in range(1, YS):
        arrived(shares.at[dy - 1], share_recv.at[dy - 1])
    rows = pl.ds(pl.multiple_of(y * SHARE, SHARE), SHARE)
    pull = pull_own[rows, :] + shares[0] + shares[1] + shares[2]
    unit = ui[pl.ds(pl.multiple_of(core * ROWS + y * SHARE, SHARE), SHARE), :]
    grad_unit = INV_TEMP * (pull - 2.0 * mates[rows, :])
    along = jnp.sum(unit * grad_unit, axis=1, keepdims=True)
    grad_ref[rows, :] = (grad_unit - unit * along) / norms[rows, :]
    for dy in range(1, YS):
        send(
            None,
            grad_ref.at[rows],
            grad_ref.at[rows],
            grad_send.at[dy - 1],
            grad_recv.at[dy - 1],
            device(dy=dy),
        )
    for dy in range(1, YS):
        from_rows = pl.ds(pl.multiple_of(lax.rem(y + YS - dy, YS) * SHARE, SHARE), SHARE)
        arrived(grad_ref.at[from_rows], grad_recv.at[dy - 1])
    for cond, copy in sent:
        if cond is None:
            copy.wait_send()
        else:
            pl.when(cond)(copy.wait_send)


def body(embeddings, partner):
    local = (partner - lax.axis_index("blk") * ROWS).reshape(1, ROWS)
    vmem = pl.BlockSpec(memory_space=pltpu.VMEM)
    dma = pltpu.SemaphoreType.DMA
    loss, grad = pl.pallas_call(
        kernel,
        out_shape=(
            jax.ShapeDtypeStruct((1, ROWS), F32),
            jax.ShapeDtypeStruct((ROWS, WIDTH), F32),
        ),
        in_specs=[vmem, vmem],
        out_specs=(vmem, vmem),
        scratch_shapes=[
            pltpu.VMEM((CORES * ROWS, WIDTH), F32),
            pltpu.VMEM((CORES * ROWS, WIDTH), BF16),
            pltpu.VMEM((CORES * ROWS, WIDTH), BF16),
            pltpu.VMEM((ROWS, 1), F32),
            pltpu.VMEM((ROWS, WIDTH), F32),
            pltpu.VMEM((8, ROWS, WIDTH), F32),
            pltpu.VMEM((8, ROWS, WIDTH), BF16),
            pltpu.VMEM((8, ROWS, WIDTH), BF16),
            pltpu.VMEM((8, CORES * ROWS, ROWS), F32),
            pltpu.VMEM((CORES * ROWS, ROWS), F32),
            pltpu.VMEM((8, CORES, 1, ROWS), F32),
            pltpu.VMEM((CORES, 1, ROWS), F32),
            pltpu.VMEM((CORES * ROWS, ROWS), F32),
            pltpu.VMEM((8, 1, ROWS), F32),
            pltpu.VMEM((ROWS, WIDTH), F32),
            pltpu.VMEM((ROWS, WIDTH), F32),
            pltpu.VMEM((ROWS, WIDTH), F32),
            pltpu.VMEM((YS - 1, SHARE, WIDTH), F32),
            dma((8, CHUNKS, 5)),
            dma((8, CHUNKS)),
            dma,
            dma((7,)),
            dma((8,)),
            dma((8,)),
            dma((8,)),
            dma,
            dma((2,)),
            dma((3,)),
            dma((3,)),
            dma((3,)),
            dma((3,)),
        ],
        compiler_params=pltpu.CompilerParams(
            collective_id=0, has_side_effects=True, vmem_limit_bytes=48 * 2**20
        ),
    )(embeddings, local)
    return loss.reshape(ROWS), grad


def solution(mesh):
    return jax.shard_map(
        body,
        mesh=mesh,
        in_specs=(P("blk", None), P("blk")),
        out_specs=(P("blk"), P("blk", None)),
        check_vma=False,
    )
```

```python
import jax
import jax.numpy as jnp
from jax import lax
from jax.experimental import pallas as pl
from jax.experimental.pallas import tpu as pltpu
from jax.sharding import PartitionSpec as P

MESH = pl.DeviceIdType.MESH
F32 = jnp.float32
BF16 = jnp.bfloat16
HIGHEST = lax.Precision.HIGHEST
INV_TEMP = 10.0
ROWS = 192
WIDTH = 256
XS, YS, ZS, CORES = 4, 4, 8, 2
HALF = ROWS // 2
SHARE = ROWS // YS
ALL = 4 * ROWS


def dot_nn(a, b, precision=None):
    return lax.dot_general(
        a, b, (((1,), (0,)), ((), ())), precision=precision, preferred_element_type=F32
    )


def dot_nt(a, b, precision=None):
    return lax.dot_general(
        a, b, (((1,), (1,)), ((), ())), precision=precision, preferred_element_type=F32
    )


def split(value):
    high = value.astype(BF16)
    return high, (value - high.astype(F32)).astype(BF16)


def kernel(
    emb_hbm,
    partner_hbm,
    loss_ref,
    grad_ref,
    emb_ref,
    partner_ref,
    ui,
    ui_hi,
    ui_lo,
    norms,
    mates,
    uj,
    uj_hi,
    uj_lo,
    weights,
    acc,
    sums,
    inverse,
    inverse_rows,
    inverse_cols,
    pull_out,
    pull_in,
    pull_own,
    shares,
    local_sem,
    z_send,
    z_recv,
    x_send,
    x_recv,
    row_send,
    row_recv,
    sums_send,
    sums_recv,
    inv_send,
    inv_recv,
    sib_send,
    sib_recv,
    share_send,
    share_recv,
    grad_send,
    grad_recv,
):
    blk = lax.axis_index("blk")
    y = lax.axis_index("rep")
    core = lax.rem(blk, CORES)
    x = lax.rem(lax.div(blk, CORES), XS)
    z = lax.div(blk, CORES * XS)
    odd = lax.rem(z, 2)
    z_pair = z + 1 - 2 * odd

    def device(dx=0, dy=0, to_z=None, dc=0):
        there = (z if to_z is None else to_z) * XS + lax.rem(x + (dx % XS), XS)
        return (there * CORES + lax.rem(core + dc, CORES), lax.rem(y + (dy % YS), YS))

    steps = (y, YS - 1 - y)
    z_to = [
        lax.rem(z + ZS + jnp.where(lax.rem(z + k, 2) == 0, k, -k), ZS) for k in steps
    ]
    z_from = [lax.rem(z + ZS + jnp.where(odd == 0, -k, k), ZS) for k in steps]

    embedding_copy = pltpu.make_async_copy(emb_hbm, emb_ref, local_sem.at[0])
    partner_copy = pltpu.make_async_copy(partner_hbm, partner_ref, local_sem.at[1])
    embedding_copy.start()
    partner_copy.start()

    group = [
        (dy, db, dc)
        for dy in range(YS)
        for db in range(2)
        for dc in range(CORES)
        if (dy, db, dc) != (0, 0, 0)
    ]
    near = [device(dy=dy, to_z=z_pair if db else z, dc=dc) for dy, db, dc in group]
    near += [device(dx=d) for d in (1, 2, 3)]
    barrier = pltpu.get_barrier_semaphore()
    for peer in near:
        pl.semaphore_signal(barrier, inc=1, device_id=peer, device_id_type=MESH)
    for k, source in zip(steps, z_from):

        @pl.when(k != 0)
        def _():
            pl.semaphore_signal(
                barrier, inc=1, device_id=device(to_z=source), device_id_type=MESH
            )

    own_at = (core * 2 + odd) * ROWS
    own_rows = pl.ds(pl.multiple_of(own_at, ROWS), ROWS)
    sib_rows = pl.ds(pl.multiple_of(((1 - core) * 2 + odd) * ROWS, ROWS), ROWS)
    pair_rows = pl.ds(pl.multiple_of((core * 2 + 1 - odd) * ROWS, ROWS), ROWS)
    last_rows = pl.ds(pl.multiple_of(((1 - core) * 2 + 1 - odd) * ROWS, ROWS), ROWS)

    embedding_copy.wait()
    emb = emb_ref[...]
    norm = jnp.sqrt(jnp.sum(emb * emb, axis=1, keepdims=True) + 1e-12)
    unit = emb / norm
    norms[...] = norm
    ui[own_rows, :] = unit
    for h, k in enumerate(steps):

        @pl.when(k == 0)
        def _():
            uj[0, h * HALF : (h + 1) * HALF] = unit[h * HALF : (h + 1) * HALF]

    pl.semaphore_wait(
        barrier, len(near) + 2 - jnp.where(jnp.logical_or(y == 0, y == YS - 1), 1, 0)
    )

    sent = []

    def send(cond, src, dst, send_sem, recv_sem, peer):
        copy = pltpu.make_async_remote_copy(
            src_ref=src,
            dst_ref=dst,
            send_sem=send_sem,
            recv_sem=recv_sem,
            device_id=peer,
            device_id_type=MESH,
        )
        if cond is None:
            copy.start()
        else:
            pl.when(cond)(copy.start)
        sent.append((cond, copy))

    def arrived(dst, recv_sem):
        pltpu.make_async_remote_copy(
            src_ref=dst,
            dst_ref=dst,
            send_sem=recv_sem,
            recv_sem=recv_sem,
            device_id=device(dc=1),
            device_id_type=MESH,
        ).wait_recv()

    def half(column, h):
        return uj.at[column, pl.ds(h * HALF, HALF)]

    def x_spread(cond, h):
        for column, dx in ((3, 2), (1, 1), (2, 3)):
            send(
                cond,
                half(0, h),
                half(column, h),
                x_send.at[column - 1, h],
                x_recv.at[column - 1, h],
                device(dx=dx),
            )

    for h, k in enumerate(steps):
        at = pl.ds(pl.multiple_of(own_at + h * HALF, HALF), HALF)
        send(k != 0, ui.at[at], half(0, h), z_send.at[h], z_recv.at[h], device(to_z=z_to[h]))
    for h, k in enumerate(steps):
        x_spread(k == 0, h)
    rows_of = ui.at[own_rows]
    send(None, rows_of, rows_of, row_send.at[0], row_recv.at[0], device(dc=1))
    send(None, rows_of, rows_of, row_send.at[1], row_recv.at[1], device(to_z=z_pair))

    def take_half(cond, h):
        @pl.when(cond)
        def _():
            arrived(half(0, h), z_recv.at[h])

        x_spread(cond, h)

    take_half(jnp.logical_or(y == 1, y == 3), 0)
    take_half(jnp.logical_or(y == 0, y == 2), 1)
    take_half(y == 2, 0)
    take_half(y == 1, 1)
    arrived(ui.at[pair_rows], row_recv.at[1])
    rows_of = ui.at[pair_rows]
    send(None, rows_of, rows_of, row_send.at[2], row_recv.at[2], device(dc=1))
    arrived(ui.at[sib_rows], row_recv.at[0])
    arrived(ui.at[last_rows], row_recv.at[2])

    def scores(column):
        high, low = split(uj[column])
        uj_hi[column] = high
        uj_lo[column] = low
        for part in range(2):
            rows = slice(part * 2 * ROWS, (part + 1) * 2 * ROWS)
            left, left_low = ui_hi[rows, :], ui_lo[rows, :]
            score = dot_nt(left, high) + dot_nt(left_low, high) + dot_nt(left, low)
            weight = jnp.exp(score * INV_TEMP - INV_TEMP)
            if column == 0:
                col = lax.broadcasted_iota(jnp.int32, (1, ROWS), 1)
                first = jnp.where(y == 0, 0, HALF)
                kept = jnp.logical_or(y == 0, y == YS - 1)
                start = jnp.where(kept, own_at - part * 2 * ROWS, 4 * ALL)
                inside = jnp.logical_and(col >= first, col < first + HALF)
                diagonal = jnp.where(inside, col + start, 4 * ALL)
                row = lax.broadcasted_iota(jnp.int32, weight.shape, 0)
                weight = jnp.where(row == diagonal, 0.0, weight)
                acc[rows, :] = weight
            else:
                acc[rows, :] += weight
            weights[column, rows, :] = weight

    high, low = split(ui[...])
    ui_hi[...] = high
    ui_lo[...] = low
    for column in range(XS):
        if column:
            for h in range(2):
                arrived(half(column, h), x_recv.at[column - 1, h])
        scores(column)

    mine = (y * 2 + odd) * CORES + core
    ones = jnp.ones((8, ROWS), F32)
    for i in range(8):
        part = acc[i * HALF : (i + 1) * HALF, :]
        sums[mine, i] = dot_nt(ones, part, HIGHEST)[0:1]
    for i, (dy, db, dc) in enumerate(group):
        send(
            None,
            sums.at[mine],
            sums.at[mine],
            sums_send.at[i],
            sums_recv.at[mine],
            device(dy=dy, to_z=z_pair if db else z, dc=dc),
        )
    partner_copy.wait()
    unit = ui[own_rows, :]
    node = lax.broadcasted_iota(jnp.int32, (ROWS, ROWS), 0)
    pairing = (node + blk * ROWS == partner_ref[...]).astype(F32)
    mate = dot_nn(pairing, unit, HIGHEST)
    mates[...] = mate
    pair_score = dot_nt(jnp.ones((8, WIDTH), F32), unit * mate, HIGHEST)[0:1]
    for dy, db, dc in group:
        other_b = 1 - odd if db else odd
        other = (lax.rem(y + dy, YS) * 2 + other_b) * CORES + lax.rem(core + dc, CORES)
        arrived(sums.at[other], sums_recv.at[other])
    total = sums[0]
    for i in range(1, 4 * YS):
        total = total + sums[i]
    inverse[...] = 1.0 / total

    for h, k in enumerate(steps):
        for column, dx in ((3, 2), (1, 1), (2, 3), (0, 0)):
            send(
                k != 0 if column == 0 else None,
                inverse.at[(core * 2 + odd) * 2 + h],
                inverse_cols.at[column, h],
                inv_send.at[column, h],
                inv_recv.at[column, h],
                device(dx=dx, to_z=z_to[h]),
            )

        @pl.when(k == 0)
        def _():
            inverse_cols[0, h] = inverse[(core * 2 + odd) * 2 + h]

    own_inverse = jnp.concatenate(
        [inverse[(core * 2 + odd) * 2], inverse[(core * 2 + odd) * 2 + 1]], axis=1
    )
    loss_ref[...] = INV_TEMP - jnp.log(own_inverse) - INV_TEMP * pair_score
    same = lax.broadcasted_iota(jnp.int32, (ROWS, ROWS), 1) == node
    for i in range(4):
        row = jnp.concatenate([inverse[2 * i], inverse[2 * i + 1]], axis=1)
        column_sum = jnp.sum(jnp.where(same, row, 0.0), axis=1, keepdims=True)
        inverse_rows[i * ROWS : (i + 1) * ROWS, :] = jnp.broadcast_to(column_sum, (ROWS, ROWS))
    for column in range(XS):
        for h, k in enumerate(steps):
            if column:
                arrived(inverse_cols.at[column, h], inv_recv.at[column, h])
            else:

                @pl.when(k != 0)
                def _():
                    arrived(inverse_cols.at[column, h], inv_recv.at[column, h])

    def pulls(first):
        rows = pl.ds(pl.multiple_of(first, 2 * ROWS), 2 * ROWS)
        total = jnp.zeros((2 * ROWS, WIDTH), F32)
        for column in range(XS):
            across = jnp.concatenate([inverse_cols[column, 0], inverse_cols[column, 1]], axis=1)
            both = weights[column, rows, :] * (inverse_rows[rows, :] + across)
            high, low = split(both)
            total = total + dot_nn(high, uj_hi[column])
            total = total + dot_nn(low, uj_hi[column])
            total = total + dot_nn(high, uj_lo[column])
        return total

    pull_out[...] = pulls((1 - core) * 2 * ROWS)
    send(None, pull_out, pull_in, sib_send, sib_recv, device(dc=1))
    pull_own[...] = pulls(core * 2 * ROWS)
    arrived(pull_in, sib_recv)
    pull_own[...] += pull_in[...]

    def share(block, at):
        return pl.ds(pl.multiple_of(block * ROWS + at * SHARE, SHARE), SHARE)

    for db in (1, 0):
        for dy in range(1 - db, YS):
            slot = dy + 3 if db else dy - 1
            send(
                None,
                pull_own.at[share(1 - odd if db else odd, lax.rem(y + dy, YS))],
                shares.at[slot],
                share_send.at[slot],
                share_recv.at[slot],
                device(dy=dy, to_z=z_pair if db else z),
            )
    for slot in range(7):
        arrived(shares.at[slot], share_recv.at[slot])
    rows = pl.ds(pl.multiple_of(y * SHARE, SHARE), SHARE)
    pull = pull_own[share(odd, y), :]
    for slot in range(7):
        pull = pull + shares[slot]
    unit = ui[pl.ds(pl.multiple_of(own_at + y * SHARE, SHARE), SHARE), :]
    grad_unit = INV_TEMP * (pull - 2.0 * mates[rows, :])
    along = jnp.sum(unit * grad_unit, axis=1, keepdims=True)
    grad_ref[rows, :] = (grad_unit - unit * along) / norms[rows, :]
    for dy in range(1, YS):
        send(
            None,
            grad_ref.at[rows],
            grad_ref.at[rows],
            grad_send.at[dy - 1],
            grad_recv.at[dy - 1],
            device(dy=dy),
        )
    for dy in range(1, YS):
        from_rows = pl.ds(pl.multiple_of(lax.rem(y + YS - dy, YS) * SHARE, SHARE), SHARE)
        arrived(grad_ref.at[from_rows], grad_recv.at[dy - 1])
    for cond, copy in sent:
        if cond is None:
            copy.wait_send()
        else:
            pl.when(cond)(copy.wait_send)


def body(embeddings, partner):
    vmem = pl.BlockSpec(memory_space=pltpu.VMEM)
    hbm = pl.BlockSpec(memory_space=pl.ANY)
    dma = pltpu.SemaphoreType.DMA
    loss, grad = pl.pallas_call(
        kernel,
        out_shape=(
            jax.ShapeDtypeStruct((1, ROWS), F32),
            jax.ShapeDtypeStruct((ROWS, WIDTH), F32),
        ),
        in_specs=[hbm, hbm],
        out_specs=(vmem, vmem),
        scratch_shapes=[
            pltpu.VMEM((ROWS, WIDTH), F32),
            pltpu.VMEM((1, ROWS), jnp.int32),
            pltpu.VMEM((ALL, WIDTH), F32),
            pltpu.VMEM((ALL, WIDTH), BF16),
            pltpu.VMEM((ALL, WIDTH), BF16),
            pltpu.VMEM((ROWS, 1), F32),
            pltpu.VMEM((ROWS, WIDTH), F32),
            pltpu.VMEM((XS, ROWS, WIDTH), F32),
            pltpu.VMEM((XS, ROWS, WIDTH), BF16),
            pltpu.VMEM((XS, ROWS, WIDTH), BF16),
            pltpu.VMEM((XS, ALL, ROWS), F32),
            pltpu.VMEM((ALL, ROWS), F32),
            pltpu.VMEM((4 * YS, 8, 1, HALF), F32),
            pltpu.VMEM((8, 1, HALF), F32),
            pltpu.VMEM((ALL, ROWS), F32),
            pltpu.VMEM((XS, 2, 1, HALF), F32),
            pltpu.VMEM((2 * ROWS, WIDTH), F32),
            pltpu.VMEM((2 * ROWS, WIDTH), F32),
            pltpu.VMEM((2 * ROWS, WIDTH), F32),
            pltpu.VMEM((7, SHARE, WIDTH), F32),
            dma((2,)),
            dma((2,)),
            dma((2,)),
            dma((3, 2)),
            dma((3, 2)),
            dma((3,)),
            dma((3,)),
            dma((15,)),
            dma((16,)),
            dma((4, 2)),
            dma((4, 2)),
            dma,
            dma,
            dma((7,)),
            dma((7,)),
            dma((3,)),
            dma((3,)),
        ],
        compiler_params=pltpu.CompilerParams(
            collective_id=0, has_side_effects=True, vmem_limit_bytes=48 * 2**20
        ),
    )(embeddings, partner.reshape(1, ROWS))
    return loss.reshape(ROWS), grad


def solution(mesh):
    return jax.shard_map(
        body,
        mesh=mesh,
        in_specs=(P("blk", None), P("blk")),
        out_specs=(P("blk"), P("blk", None)),
        check_vma=False,
    )
```

```python
import functools

import jax
import jax.numpy as jnp
from jax import lax
from jax.experimental import pallas as pl
from jax.experimental.pallas import tpu as pltpu
from jax.sharding import PartitionSpec as P

MESH = pl.DeviceIdType.MESH
F32 = jnp.float32
BF16 = jnp.bfloat16
HIGHEST = lax.Precision.HIGHEST
INV_TEMP = 10.0
ROWS = 192
WIDTH = 256
XS, YS, ZS, CORES = 4, 4, 8, 2
QUARTER = ROWS // 4
SHARE = ROWS // YS
TILE = 128
PLACE = (0, 2, 1, 3)
ALL = 4 * ROWS


def dot_nn(a, b, precision=None):
    return lax.dot_general(
        a, b, (((1,), (0,)), ((), ())), precision=precision, preferred_element_type=F32
    )


def dot_nt(a, b, precision=None):
    return lax.dot_general(
        a, b, (((1,), (1,)), ((), ())), precision=precision, preferred_element_type=F32
    )


def split(value):
    high = value.astype(BF16)
    return high, (value - high.astype(F32)).astype(BF16)


def kernel(
    emb_hbm,
    partner_hbm,
    loss_ref,
    grad_ref,
    emb_ref,
    partner_ref,
    ui,
    ui_wide,
    norms,
    mates,
    uj,
    transit,
    uj_wide,
    uj_tall,
    weights,
    acc,
    sums,
    inverse,
    inverse_own,
    inverse_rows,
    inverse_cols,
    across,
    wide,
    pull_out,
    pull_in,
    pull_own,
    shares,
    local_sem,
    z_send,
    z_recv,
    x_send,
    x_recv,
    row_send,
    row_recv,
    sums_send,
    sums_recv,
    inv_send,
    inv_recv,
    sib_send,
    sib_recv,
    share_send,
    share_recv,
    grad_send,
    grad_recv,
):
    blk = lax.axis_index("blk")
    y = lax.axis_index("rep")
    core = lax.rem(blk, CORES)
    x = lax.rem(lax.div(blk, CORES), XS)
    z = lax.div(blk, CORES * XS)
    odd = lax.rem(z, 2)
    z_pair = z + 1 - 2 * odd

    def device(dx=0, dy=0, to_z=None, dc=0):
        there = (z if to_z is None else to_z) * XS + lax.rem(x + (dx % XS), XS)
        return (there * CORES + lax.rem(core + dc, CORES), lax.rem(y + (dy % YS), YS))

    quarters = [lax.rem(k + YS - y, 4) for k in range(4)]
    z_to = [
        lax.rem(z + ZS + jnp.where(lax.rem(z + k, 2) == 0, k, -k), ZS) for k in range(4)
    ]
    z_from = [lax.rem(z + ZS + jnp.where(odd == 0, -k, k), ZS) for k in range(4)]

    embedding_copy = pltpu.make_async_copy(emb_hbm, emb_ref, local_sem.at[0])
    partner_copy = pltpu.make_async_copy(partner_hbm, partner_ref, local_sem.at[1])
    embedding_copy.start()
    partner_copy.start()

    group = [
        (dy, db, dc)
        for dy in range(YS)
        for db in range(2)
        for dc in range(CORES)
        if (dy, db, dc) != (0, 0, 0)
    ]
    near = [device(dc=1), device(to_z=z_pair)]
    near += [device(dx=d) for d in (1, 2, 3)] + [device(dy=d) for d in (1, 2, 3)]
    near += [device(to_z=z_from[k]) for k in (1, 2, 3)]
    barrier = pltpu.get_barrier_semaphore()
    for peer in near:
        pl.semaphore_signal(barrier, inc=1, device_id=peer, device_id_type=MESH)
    own_at = (core * 2 + odd) * ROWS
    own_rows = pl.ds(pl.multiple_of(own_at, ROWS), ROWS)
    sib_rows = pl.ds(pl.multiple_of(((1 - core) * 2 + odd) * ROWS, ROWS), ROWS)
    pair_rows = pl.ds(pl.multiple_of((core * 2 + 1 - odd) * ROWS, ROWS), ROWS)
    last_rows = pl.ds(pl.multiple_of(((1 - core) * 2 + 1 - odd) * ROWS, ROWS), ROWS)

    embedding_copy.wait()
    emb = emb_ref[...]
    norm = jnp.sqrt(jnp.sum(emb * emb, axis=1, keepdims=True) + 1e-12)
    unit = emb / norm
    norms[...] = norm
    ui[own_rows, :] = unit
    first = pl.ds(pl.multiple_of(own_at + quarters[0] * QUARTER, QUARTER), QUARTER)
    uj[0:QUARTER, :] = ui[first, :]
    second = pl.ds(pl.multiple_of(own_at + quarters[1] * QUARTER, QUARTER), QUARTER)
    transit[0:QUARTER, :] = ui[second, :]

    pl.semaphore_wait(barrier, len(near))

    sent = []

    def send(src, dst, send_sem, recv_sem, peer):
        copy = pltpu.make_async_remote_copy(
            src_ref=src,
            dst_ref=dst,
            send_sem=send_sem,
            recv_sem=recv_sem,
            device_id=peer,
            device_id_type=MESH,
        )
        copy.start()
        sent.append(copy)

    def settle():
        for copy in sent:
            copy.wait_send()
        sent.clear()

    def arrived(dst, recv_sem):
        pltpu.make_async_remote_copy(
            src_ref=dst,
            dst_ref=dst,
            send_sem=recv_sem,
            recv_sem=recv_sem,
            device_id=device(dc=1),
            device_id_type=MESH,
        ).wait_recv()

    def quarter(k, column):
        return uj.at[pl.ds(PLACE[k] * ROWS + column * QUARTER, QUARTER)]

    def x_spread(k, place):
        for column, dx in ((3, 2), (1, 1), (2, 3)):
            send(
                place(0),
                place(column),
                x_send.at[k, column - 1],
                x_recv.at[k, column - 1],
                device(dx=dx),
            )

    def in_transit(column):
        return transit.at[pl.ds(column * QUARTER, QUARTER)]

    def x_arrived(k, place):
        for column in range(1, XS):
            arrived(place(column), x_recv.at[k, column - 1])

    for k in (3, 2):
        at = pl.ds(pl.multiple_of(own_at + quarters[k] * QUARTER, QUARTER), QUARTER)
        send(ui.at[at], quarter(k, 0), z_send.at[k - 1], z_recv.at[k - 1], device(to_z=z_to[k]))
    x_spread(1, in_transit)
    x_spread(0, functools.partial(quarter, 0))
    rows_of = ui.at[own_rows]
    send(rows_of, rows_of, row_send.at[0], row_recv.at[0], device(dc=1))
    send(rows_of, rows_of, row_send.at[1], row_recv.at[1], device(to_z=z_pair))
    arrived(quarter(2, 0), z_recv.at[1])
    x_spread(2, functools.partial(quarter, 2))
    x_arrived(1, in_transit)
    near_place = uj.at[pl.ds(PLACE[1] * ROWS, ROWS)]
    send(transit, near_place, z_send.at[0], z_recv.at[0], device(to_z=z_to[1]))
    arrived(quarter(3, 0), z_recv.at[2])
    x_spread(3, functools.partial(quarter, 3))
    arrived(ui.at[pair_rows], row_recv.at[1])
    rows_of = ui.at[pair_rows]
    send(rows_of, rows_of, row_send.at[2], row_recv.at[2], device(dc=1))
    arrived(ui.at[sib_rows], row_recv.at[0])
    arrived(ui.at[last_rows], row_recv.at[2])

    def scores(start, stop):
        high, low = split(uj[start:stop, :])
        for i, value in enumerate((high, high, low)):
            uj_wide[start:stop, i * WIDTH : (i + 1) * WIDTH] = value
            uj_tall[i * ALL + start : i * ALL + stop, :] = value
        score = dot_nt(ui_wide[...], uj_wide[start:stop, :])
        weight = jnp.exp(score * INV_TEMP - INV_TEMP)
        if start == 0:
            col = lax.broadcasted_iota(jnp.int32, (1, stop), 1)
            diagonal = jnp.where(col < QUARTER, col + own_at + quarters[0] * QUARTER, 4 * ALL)
            row = lax.broadcasted_iota(jnp.int32, weight.shape, 0)
            weight = jnp.where(row == diagonal, 0.0, weight)
        weights[:, start:stop] = weight
        tiles = [weight[:, i : i + TILE] for i in range(0, stop - start, TILE)]
        part = tiles[0]
        for tile in tiles[1:]:
            part = part + tile
        if start == 0:
            acc[...] = part
        else:
            acc[...] += part

    high, low = split(ui[...])
    for i, value in enumerate((high, low, high)):
        ui_wide[:, i * WIDTH : (i + 1) * WIDTH] = value
    x_arrived(0, functools.partial(quarter, 0))
    x_arrived(2, functools.partial(quarter, 2))
    scores(0, 384)
    arrived(near_place, z_recv.at[0])
    scores(384, 512)
    x_arrived(3, functools.partial(quarter, 3))
    scores(512, 768)

    gather_sent = list(sent)
    sent.clear()
    mine = (y * 2 + odd) * CORES + core
    ones = jnp.ones((8, TILE), BF16)
    for i in range(4):
        high, low = split(acc[i * ROWS : (i + 1) * ROWS, :])
        sums[mine, i] = (dot_nt(ones, high) + dot_nt(ones, low))[0:1]
    for i, (dy, db, dc) in enumerate(group):
        send(
            sums.at[mine],
            sums.at[mine],
            sums_send.at[i],
            sums_recv.at[mine],
            device(dy=dy, to_z=z_pair if db else z, dc=dc),
        )
    partner_copy.wait()
    unit = ui[own_rows, :]
    node = lax.broadcasted_iota(jnp.int32, (ROWS, ROWS), 0)
    pairing = (node + blk * ROWS == partner_ref[...]).astype(F32)
    mate = dot_nn(pairing, unit, HIGHEST)
    mates[...] = mate
    pair_score = dot_nt(jnp.ones((8, WIDTH), F32), unit * mate, HIGHEST)[0:1]
    sums_sent = list(sent)
    sent[:] = gather_sent
    settle()
    for dy, db, dc in group:
        other_b = 1 - odd if db else odd
        other = (lax.rem(y + dy, YS) * 2 + other_b) * CORES + lax.rem(core + dc, CORES)
        arrived(sums.at[other], sums_recv.at[other])
    total = sums[0]
    for i in range(1, 4 * YS):
        total = total + sums[i]
    inverse[...] = 1.0 / total

    own_inverse = inverse[core * 2 + odd]
    for i in range(4):
        inverse_own[i] = own_inverse[:, i * QUARTER : (i + 1) * QUARTER]

    for k in (3, 2, 1, 0):
        for column, dx in ((3, 2), (1, 1), (2, 3), (0, 0)):
            if (k, column) != (0, 0):
                send(
                    inverse_own.at[quarters[k]],
                    inverse_cols.at[k, column],
                    inv_send.at[k, column],
                    inv_recv.at[k, column],
                    device(dx=dx, to_z=z_to[k]),
                )
    inverse_cols[0, 0] = inverse_own[quarters[0]]
    loss_ref[...] = INV_TEMP - jnp.log(own_inverse) - INV_TEMP * pair_score
    same = lax.broadcasted_iota(jnp.int32, (ROWS, ROWS), 1) == node
    for i in range(4):
        column_sum = jnp.sum(jnp.where(same, inverse[i], 0.0), axis=1, keepdims=True)
        inverse_rows[i * ROWS : (i + 1) * ROWS, :] = jnp.broadcast_to(column_sum, (ROWS, TILE))
    inverse_sent = list(sent)
    sent[:] = sums_sent
    settle()
    for k in range(4):
        for column in range(XS):
            if (k, column) != (0, 0):
                arrived(inverse_cols.at[k, column], inv_recv.at[k, column])
    across[...] = jnp.concatenate(
        [inverse_cols[k, column] for k in PLACE for column in range(XS)], axis=1
    )

    def pulls(part, block):
        rows = pl.ds(pl.multiple_of(block * ROWS, ROWS), ROWS)
        for start in range(0, ALL, TILE):
            tile = slice(start, start + TILE)
            both = weights[rows, tile] * (inverse_rows[rows, :] + across[:, tile])
            high, low = split(both)
            for i, value in enumerate((high, low, high)):
                wide[part, :, i * ALL + start : i * ALL + start + TILE] = value
        return dot_nn(wide[part], uj_tall[...])

    there = (1 - odd, odd)
    for i in range(2):
        pull_out[i] = pulls(i, (1 - core) * 2 + there[i])
        send(pull_out.at[i], pull_in.at[i], sib_send.at[i], sib_recv.at[i], device(dc=1))
    for i in range(2):
        pull_own[i] = pulls(2 + i, core * 2 + there[i])

    def share(at):
        return pl.ds(pl.multiple_of(at * SHARE, SHARE), SHARE)

    for i in range(2):
        arrived(pull_in.at[i], sib_recv.at[i])
        pull_own[i] += pull_in[i]
        for dy in range(i, YS):
            slot = dy - 1 if i else dy + 3
            send(
                pull_own.at[i, share(lax.rem(y + dy, YS))],
                shares.at[slot],
                share_send.at[slot],
                share_recv.at[slot],
                device(dy=dy, to_z=z if i else z_pair),
            )
    shares_sent = list(sent)
    sent[:] = inverse_sent
    settle()
    for slot in range(7):
        arrived(shares.at[slot], share_recv.at[slot])
    rows = pl.ds(pl.multiple_of(y * SHARE, SHARE), SHARE)
    pull = pull_own[1, share(y), :]
    for slot in range(7):
        pull = pull + shares[slot]
    unit = ui[pl.ds(pl.multiple_of(own_at + y * SHARE, SHARE), SHARE), :]
    grad_unit = INV_TEMP * (pull - 2.0 * mates[rows, :])
    along = jnp.sum(unit * grad_unit, axis=1, keepdims=True)
    grad_ref[rows, :] = (grad_unit - unit * along) / norms[rows, :]
    for dy in range(1, YS):
        send(
            grad_ref.at[rows],
            grad_ref.at[rows],
            grad_send.at[dy - 1],
            grad_recv.at[dy - 1],
            device(dy=dy),
        )
    sent.extend(shares_sent)
    settle()
    for dy in range(1, YS):
        from_rows = pl.ds(pl.multiple_of(lax.rem(y + YS - dy, YS) * SHARE, SHARE), SHARE)
        arrived(grad_ref.at[from_rows], grad_recv.at[dy - 1])
    settle()


def body(embeddings, partner):
    vmem = pl.BlockSpec(memory_space=pltpu.VMEM)
    hbm = pl.BlockSpec(memory_space=pltpu.HBM)
    dma = pltpu.SemaphoreType.DMA
    loss, grad = pl.pallas_call(
        kernel,
        out_shape=(
            jax.ShapeDtypeStruct((1, ROWS), F32),
            jax.ShapeDtypeStruct((ROWS, WIDTH), F32),
        ),
        in_specs=[hbm, hbm],
        out_specs=(vmem, vmem),
        scratch_shapes=[
            pltpu.VMEM((ROWS, WIDTH), F32),
            pltpu.VMEM((1, ROWS), jnp.int32),
            pltpu.VMEM((ALL, WIDTH), F32),
            pltpu.VMEM((ALL, 3 * WIDTH), BF16),
            pltpu.VMEM((ROWS, 1), F32),
            pltpu.VMEM((ROWS, WIDTH), F32),
            pltpu.VMEM((ALL, WIDTH), F32),
            pltpu.VMEM((ROWS, WIDTH), F32),
            pltpu.VMEM((ALL, 3 * WIDTH), BF16),
            pltpu.VMEM((3 * ALL, WIDTH), BF16),
            pltpu.VMEM((ALL, ALL), F32),
            pltpu.VMEM((ALL, TILE), F32),
            pltpu.VMEM((4 * YS, 4, 1, ROWS), F32),
            pltpu.VMEM((4, 1, ROWS), F32),
            pltpu.VMEM((4, 1, QUARTER), F32),
            pltpu.VMEM((ALL, TILE), F32),
            pltpu.VMEM((4, XS, 1, QUARTER), F32),
            pltpu.VMEM((1, ALL), F32),
            pltpu.VMEM((4, ROWS, 3 * ALL), BF16),
            pltpu.VMEM((2, ROWS, WIDTH), F32),
            pltpu.VMEM((2, ROWS, WIDTH), F32),
            pltpu.VMEM((2, ROWS, WIDTH), F32),
            pltpu.VMEM((7, SHARE, WIDTH), F32),
            dma((2,)),
            dma((3,)),
            dma((3,)),
            dma((4, 3)),
            dma((4, 3)),
            dma((3,)),
            dma((3,)),
            dma((15,)),
            dma((16,)),
            dma((4, 4)),
            dma((4, 4)),
            dma((2,)),
            dma((2,)),
            dma((7,)),
            dma((7,)),
            dma((3,)),
            dma((3,)),
        ],
        compiler_params=pltpu.CompilerParams(
            collective_id=0, has_side_effects=True, vmem_limit_bytes=56254464
        ),
    )(embeddings, partner.reshape(1, ROWS))
    return loss.reshape(ROWS), grad


def solution(mesh):
    return jax.shard_map(
        body,
        mesh=mesh,
        in_specs=(P("blk", None), P("blk")),
        out_specs=(P("blk"), P("blk", None)),
        check_vma=False,
    )
```

```python
import math

import jax
import jax.numpy as jnp
from jax import lax
from jax.experimental import pallas as pl
from jax.experimental.pallas import tpu as pltpu
from jax.sharding import PartitionSpec as P

MESH = pl.DeviceIdType.MESH
F32 = jnp.float32
BF16 = jnp.bfloat16
HIGHEST = lax.Precision.HIGHEST
INV_TEMP = 10.0
EXP_SCALE = INV_TEMP * math.log2(math.e)
ROWS = 192
WIDTH = 256
XS, YS, ZS, CORES = 4, 4, 8, 2
QUARTER = ROWS // 4
SHARE = ROWS // YS
TILE = 128
ALL = 4 * ROWS


def dot_nn(a, b, precision=None):
    return lax.dot_general(
        a, b, (((1,), (0,)), ((), ())), precision=precision, preferred_element_type=F32
    )


def dot_nt(a, b, precision=None):
    return lax.dot_general(
        a, b, (((1,), (1,)), ((), ())), precision=precision, preferred_element_type=F32
    )


def split(value):
    high = value.astype(BF16)
    return high, (value - high.astype(F32)).astype(BF16)


def kernel(
    emb_hbm,
    partner_hbm,
    loss_ref,
    grad_ref,
    emb_ref,
    partner_ref,
    ui,
    ui_wide,
    norms,
    mates,
    pair_scores,
    uj,
    uj_wide,
    uj_tall,
    weights,
    acc,
    sums,
    inverse,
    inverse_own,
    inverse_rows,
    inverse_cols,
    across,
    wide,
    pull_first,
    pull_out,
    pull_in,
    pull_own,
    shares,
    local_sem,
    x_send,
    x_recv,
    row_send,
    row_recv,
    sums_send,
    sums_recv,
    inv_send,
    inv_recv,
    sib_send,
    sib_recv,
    share_send,
    share_recv,
    grad_send,
    grad_recv,
):
    blk = lax.axis_index("blk")
    y = lax.axis_index("rep")
    core = lax.rem(blk, CORES)
    x = lax.rem(lax.div(blk, CORES), XS)
    z = lax.div(blk, CORES * XS)
    odd = lax.rem(z, 2)
    z_pair = z + 1 - 2 * odd

    def device(dx=0, dy=0, to_z=None, dc=0):
        there = (z if to_z is None else to_z) * XS + lax.rem(x + (dx % XS), XS)
        return (there * CORES + lax.rem(core + dc, CORES), lax.rem(y + (dy % YS), YS))

    quarters = [lax.rem(k + YS - y, 4) for k in range(4)]
    z_to = [
        lax.rem(z + ZS + jnp.where(lax.rem(z + k, 2) == 0, k, -k), ZS) for k in range(4)
    ]
    z_from = [lax.rem(z + ZS + jnp.where(odd == 0, -k, k), ZS) for k in range(4)]

    embedding_copy = pltpu.make_async_copy(emb_hbm, emb_ref, local_sem.at[0])
    partner_copy = pltpu.make_async_copy(partner_hbm, partner_ref, local_sem.at[1])
    embedding_copy.start()
    partner_copy.start()

    group = [
        (dy, db, dc)
        for dy in range(YS)
        for db in range(2)
        for dc in range(CORES)
        if (dy, db, dc) != (0, 0, 0)
    ]
    group.sort(key=lambda to: -(min(to[0], YS - to[0]) + to[1]))
    near = [device(dc=1), device(to_z=z_pair)]
    near += [device(dx=d) for d in (1, 2, 3)] + [device(dy=d) for d in (1, 2, 3)]
    near += [device(to_z=z_from[k]) for k in (1, 2, 3)]
    near += [device(dx=d, to_z=z_from[1]) for d in (1, 2, 3)]
    barrier = pltpu.get_barrier_semaphore()
    for peer in near:
        pl.semaphore_signal(barrier, inc=1, device_id=peer, device_id_type=MESH)
    own_at = (core * 2 + odd) * ROWS
    own_rows = pl.ds(pl.multiple_of(own_at, ROWS), ROWS)
    sib_rows = pl.ds(pl.multiple_of(((1 - core) * 2 + odd) * ROWS, ROWS), ROWS)
    pair_rows = pl.ds(pl.multiple_of((core * 2 + 1 - odd) * ROWS, ROWS), ROWS)
    last_rows = pl.ds(pl.multiple_of(((1 - core) * 2 + 1 - odd) * ROWS, ROWS), ROWS)

    embedding_copy.wait()
    emb = emb_ref[...]
    norm = jnp.sqrt(jnp.sum(emb * emb, axis=1, keepdims=True) + 1e-12)
    unit = emb / norm
    norms[...] = norm
    ui[own_rows, :] = unit
    first = pl.ds(pl.multiple_of(own_at + quarters[0] * QUARTER, QUARTER), QUARTER)
    uj[0:QUARTER, :] = ui[first, :]
    pl.semaphore_wait(barrier, len(near))

    sent = []

    def send(src, dst, send_sem, recv_sem, peer):
        copy = pltpu.make_async_remote_copy(
            src_ref=src,
            dst_ref=dst,
            send_sem=send_sem,
            recv_sem=recv_sem,
            device_id=peer,
            device_id_type=MESH,
        )
        copy.start()
        sent.append(copy)

    def settle():
        for copy in sent:
            copy.wait_send()
        sent.clear()

    def arrived(dst, recv_sem):
        pltpu.make_async_remote_copy(
            src_ref=dst,
            dst_ref=dst,
            send_sem=recv_sem,
            recv_sem=recv_sem,
            device_id=device(dc=1),
            device_id_type=MESH,
        ).wait_recv()

    def quarter(k, column):
        return uj.at[pl.ds(k * ROWS + column * QUARTER, QUARTER)]

    around = ((3, 2), (1, 1), (2, 3))

    def x_spread(k):
        for column, dx in around:
            send(
                quarter(k, 0),
                quarter(k, column),
                x_send.at[k, column],
                x_recv.at[k, column],
                device(dx=dx),
            )

    def own_quarter(k):
        at = own_at + quarters[k] * QUARTER
        return ui.at[pl.ds(pl.multiple_of(at, QUARTER), QUARTER)]

    for k in (3, 2):
        send(own_quarter(k), quarter(k, 0), x_send.at[k, 0], x_recv.at[k, 0], device(to_z=z_to[k]))
    for column, dx in around + ((0, 0),):
        send(
            own_quarter(1),
            quarter(1, column),
            x_send.at[1, column],
            x_recv.at[1, column],
            device(dx=dx, to_z=z_to[1]),
        )
    x_spread(0)
    rows_of = ui.at[own_rows]
    send(rows_of, rows_of, row_send.at[0], row_recv.at[0], device(dc=1))
    send(rows_of, rows_of, row_send.at[1], row_recv.at[1], device(to_z=z_pair))
    partner_copy.wait()
    unit = ui[own_rows, :]
    node = lax.broadcasted_iota(jnp.int32, (ROWS, ROWS), 0)
    pairing = (node + blk * ROWS == partner_ref[...]).astype(F32)
    mate = dot_nn(pairing, unit, HIGHEST)
    mates[...] = mate
    pair_scores[...] = dot_nt(jnp.ones((8, WIDTH), F32), unit * mate, HIGHEST)[0:1]
    for k in (2, 3):
        arrived(quarter(k, 0), x_recv.at[k, 0])
        x_spread(k)
    arrived(ui.at[pair_rows], row_recv.at[1])
    rows_of = ui.at[pair_rows]
    send(rows_of, rows_of, row_send.at[2], row_recv.at[2], device(dc=1))
    arrived(ui.at[sib_rows], row_recv.at[0])
    arrived(ui.at[last_rows], row_recv.at[2])

    def scores(start, stop):
        high, low = split(uj[start:stop, :])
        for i, value in enumerate((high, high, low)):
            uj_wide[start:stop, i * WIDTH : (i + 1) * WIDTH] = value
            half = ALL // 2
            at = i * half + start % half
            uj_tall[start // half, at : at + stop - start, :] = value
        score = dot_nt(ui_wide[...], uj_wide[start:stop, :])
        weight = jnp.exp2(score * EXP_SCALE - EXP_SCALE)
        if start == 0:
            col = lax.broadcasted_iota(jnp.int32, (1, stop), 1)
            diagonal = jnp.where(col < QUARTER, col + own_at + quarters[0] * QUARTER, 4 * ALL)
            row = lax.broadcasted_iota(jnp.int32, weight.shape, 0)
            weight = jnp.where(row == diagonal, 0.0, weight)
        weights[:, start:stop] = weight
        tiles = [weight[:, i : i + TILE] for i in range(0, stop - start, TILE)]
        part = tiles[0]
        for tile in tiles[1:]:
            part = part + tile
        if start == 0:
            acc[...] = part
        else:
            acc[...] += part

    high, low = split(ui[...])
    for i, value in enumerate((high, low, high)):
        ui_wide[:, i * WIDTH : (i + 1) * WIDTH] = value
    def await_columns(k, start):
        for column in range(start, XS):
            arrived(quarter(k, column), x_recv.at[k, column])

    await_columns(0, 1)
    await_columns(1, 0)
    scores(0, 384)
    await_columns(2, 1)
    scores(384, 512)
    await_columns(3, 1)
    scores(512, 768)

    gather_sent = list(sent)
    sent.clear()
    mine = (y * 2 + odd) * CORES + core
    ones = jnp.ones((8, TILE), BF16)
    for i in range(4):
        high, low = split(acc[i * ROWS : (i + 1) * ROWS, :])
        sums[mine, i] = (dot_nt(ones, high) + dot_nt(ones, low))[0:1]
    for i, (dy, db, dc) in enumerate(group):
        send(
            sums.at[mine],
            sums.at[mine],
            sums_send.at[i],
            sums_recv.at[mine],
            device(dy=dy, to_z=z_pair if db else z, dc=dc),
        )
    sums_sent = list(sent)
    sent[:] = gather_sent
    settle()
    for dy, db, dc in group:
        other_b = 1 - odd if db else odd
        other = (lax.rem(y + dy, YS) * 2 + other_b) * CORES + lax.rem(core + dc, CORES)
        arrived(sums.at[other], sums_recv.at[other])
    total = sums[0]
    for i in range(1, 4 * YS):
        total = total + sums[i]
    inverse[...] = 1.0 / total

    own_inverse = inverse[core * 2 + odd]
    for i in range(4):
        inverse_own[i] = own_inverse[:, i * QUARTER : (i + 1) * QUARTER]

    for k in (3, 2, 1, 0):
        for column, dx in ((3, 2), (1, 1), (2, 3), (0, 0)):
            if (k, column) != (0, 0):
                send(
                    inverse_own.at[quarters[k]],
                    inverse_cols.at[k, column],
                    inv_send.at[k, column],
                    inv_recv.at[k, column],
                    device(dx=dx, to_z=z_to[k]),
                )
    inverse_cols[0, 0] = inverse_own[quarters[0]]
    loss_ref[...] = INV_TEMP - jnp.log(own_inverse) - INV_TEMP * pair_scores[...]
    same = lax.broadcasted_iota(jnp.int32, (ROWS, ROWS), 1) == node
    for i in range(4):
        column_sum = jnp.sum(jnp.where(same, inverse[i], 0.0), axis=1, keepdims=True)
        inverse_rows[i * ROWS : (i + 1) * ROWS, :] = jnp.broadcast_to(column_sum, (ROWS, TILE))
    inverse_sent = list(sent)
    sent[:] = sums_sent
    settle()
    def take_inverse(part):
        columns = slice(part * ALL // 2, (part + 1) * ALL // 2)
        pieces = []
        for k in (2 * part, 2 * part + 1):
            for column in range(XS):
                if (k, column) != (0, 0):
                    arrived(inverse_cols.at[k, column], inv_recv.at[k, column])
                pieces.append((k, column))
        across[:, columns] = jnp.concatenate([inverse_cols[piece] for piece in pieces], axis=1)

    def pulls(slot, block, part):
        rows = pl.ds(pl.multiple_of(block * ROWS, ROWS), ROWS)
        size = ALL // 2
        for start in range(0, size, TILE):
            tile = slice(part * size + start, part * size + start + TILE)
            both = weights[rows, tile] * (inverse_rows[rows, :] + across[:, tile])
            high, low = split(both)
            for i, value in enumerate((high, low, high)):
                wide[slot, :, i * size + start : i * size + start + TILE] = value
        return dot_nn(wide[slot], uj_tall[part])

    there = (1 - odd, odd)
    blocks = [(1 - core) * 2 + b for b in there] + [core * 2 + b for b in there]
    take_inverse(0)
    for i, block in enumerate(blocks):
        pull_first[i] = pulls(i, block, 0)
    take_inverse(1)

    for i in range(2):
        pull_out[i] = pull_first[i] + pulls(i, blocks[i], 1)
        send(pull_out.at[i], pull_in.at[i], sib_send.at[i], sib_recv.at[i], device(dc=1))
    for i in range(2):
        pull_own[i] = pull_first[2 + i] + pulls(2 + i, blocks[2 + i], 1)

    def share(at):
        return pl.ds(pl.multiple_of(at * SHARE, SHARE), SHARE)

    for i in range(2):
        arrived(pull_in.at[i], sib_recv.at[i])
        pull_own[i] += pull_in[i]
        for dy in (2, 1, 3) if i else (2, 1, 3, 0):
            slot = dy - 1 if i else dy + 3
            send(
                pull_own.at[i, share(lax.rem(y + dy, YS))],
                shares.at[slot],
                share_send.at[slot],
                share_recv.at[slot],
                device(dy=dy, to_z=z if i else z_pair),
            )
    shares_sent = list(sent)
    sent[:] = inverse_sent
    settle()
    for slot in range(7):
        arrived(shares.at[slot], share_recv.at[slot])
    rows = pl.ds(pl.multiple_of(y * SHARE, SHARE), SHARE)
    pull = pull_own[1, share(y), :]
    for slot in range(7):
        pull = pull + shares[slot]
    unit = ui[pl.ds(pl.multiple_of(own_at + y * SHARE, SHARE), SHARE), :]
    grad_unit = INV_TEMP * (pull - 2.0 * mates[rows, :])
    along = jnp.sum(unit * grad_unit, axis=1, keepdims=True)
    grad_ref[rows, :] = (grad_unit - unit * along) / norms[rows, :]
    for dy in (2, 1, 3):
        send(
            grad_ref.at[rows],
            grad_ref.at[rows],
            grad_send.at[dy - 1],
            grad_recv.at[dy - 1],
            device(dy=dy),
        )
    sent.extend(shares_sent)
    settle()
    for dy in range(1, YS):
        from_rows = pl.ds(pl.multiple_of(lax.rem(y + YS - dy, YS) * SHARE, SHARE), SHARE)
        arrived(grad_ref.at[from_rows], grad_recv.at[dy - 1])
    settle()


def body(embeddings, partner):
    vmem = pl.BlockSpec(memory_space=pltpu.VMEM)
    hbm = pl.BlockSpec(memory_space=pltpu.HBM)
    dma = pltpu.SemaphoreType.DMA
    loss, grad = pl.pallas_call(
        kernel,
        out_shape=(
            jax.ShapeDtypeStruct((1, ROWS), F32),
            jax.ShapeDtypeStruct((ROWS, WIDTH), F32),
        ),
        in_specs=[hbm, hbm],
        out_specs=(vmem, vmem),
        scratch_shapes=[
            pltpu.VMEM((ROWS, WIDTH), F32),
            pltpu.VMEM((1, ROWS), jnp.int32),
            pltpu.VMEM((ALL, WIDTH), F32),
            pltpu.VMEM((ALL, 3 * WIDTH), BF16),
            pltpu.VMEM((ROWS, 1), F32),
            pltpu.VMEM((ROWS, WIDTH), F32),
            pltpu.VMEM((1, ROWS), F32),
            pltpu.VMEM((ALL, WIDTH), F32),
            pltpu.VMEM((ALL, 3 * WIDTH), BF16),
            pltpu.VMEM((2, 3 * ALL // 2, WIDTH), BF16),
            pltpu.VMEM((ALL, ALL), F32),
            pltpu.VMEM((ALL, TILE), F32),
            pltpu.VMEM((4 * YS, 4, 1, ROWS), F32),
            pltpu.VMEM((4, 1, ROWS), F32),
            pltpu.VMEM((4, 1, QUARTER), F32),
            pltpu.VMEM((ALL, TILE), F32),
            pltpu.VMEM((4, XS, 1, QUARTER), F32),
            pltpu.VMEM((1, ALL), F32),
            pltpu.VMEM((4, ROWS, 3 * ALL // 2), BF16),
            pltpu.VMEM((4, ROWS, WIDTH), F32),
            pltpu.VMEM((2, ROWS, WIDTH), F32),
            pltpu.VMEM((2, ROWS, WIDTH), F32),
            pltpu.VMEM((2, ROWS, WIDTH), F32),
            pltpu.VMEM((7, SHARE, WIDTH), F32),
            dma((2,)),
            dma((4, 4)),
            dma((4, 4)),
            dma((3,)),
            dma((3,)),
            dma((15,)),
            dma((16,)),
            dma((4, 4)),
            dma((4, 4)),
            dma((2,)),
            dma((2,)),
            dma((7,)),
            dma((7,)),
            dma((3,)),
            dma((3,)),
        ],
        compiler_params=pltpu.CompilerParams(
            collective_id=0, has_side_effects=True, vmem_limit_bytes=56254464
        ),
    )(embeddings, partner.reshape(1, ROWS))
    def write(loss_vmem, grad_vmem, loss_out, grad_out, sems):
        copies = [
            pltpu.make_async_copy(grad_vmem, grad_out, sems.at[0]),
            pltpu.make_async_copy(loss_vmem, loss_out, sems.at[1]),
        ]
        for copy in copies:
            copy.start()
        for copy in copies:
            copy.wait()

    loss, grad = pl.pallas_call(
        write,
        out_shape=(
            jax.ShapeDtypeStruct((1, ROWS), F32),
            jax.ShapeDtypeStruct((ROWS, WIDTH), F32),
        ),
        in_specs=[pl.BlockSpec(memory_space=pl.ANY)] * 2,
        out_specs=(hbm, hbm),
        scratch_shapes=[dma((2,))],
        compiler_params=pltpu.CompilerParams(vmem_limit_bytes=2**20),
    )(loss, grad)
    return loss.reshape(ROWS), grad


def solution(mesh):
    return jax.shard_map(
        body,
        mesh=mesh,
        in_specs=(P("blk", None), P("blk")),
        out_specs=(P("blk"), P("blk", None)),
        check_vma=False,
    )
```

```python
import functools
import math

import jax
import jax.numpy as jnp
from jax import lax
from jax.experimental import pallas as pl
from jax.experimental.pallas import tpu as pltpu
from jax.sharding import PartitionSpec as P

MESH = pl.DeviceIdType.MESH
F32 = jnp.float32
BF16 = jnp.bfloat16
HIGHEST = lax.Precision.HIGHEST
INV_TEMP = 10.0
EXP_SCALE = INV_TEMP * math.log2(math.e)
ROWS = 192
WIDTH = 256
XS, YS, ZS, CORES = 4, 4, 8, 2
QUARTER = ROWS // 4
SHARE = ROWS // YS
TILE = 128
PLACE = (0, 2, 1, 3)
ALL = 4 * ROWS


def dot_nn(a, b, precision=None):
    return lax.dot_general(
        a, b, (((1,), (0,)), ((), ())), precision=precision, preferred_element_type=F32
    )


def dot_nt(a, b, precision=None):
    return lax.dot_general(
        a, b, (((1,), (1,)), ((), ())), precision=precision, preferred_element_type=F32
    )


def split(value):
    high = value.astype(BF16)
    return high, (value - high.astype(F32)).astype(BF16)


def kernel(
    emb_hbm,
    partner_hbm,
    loss_ref,
    grad_ref,
    emb_ref,
    partner_ref,
    ui,
    ui_wide,
    norms,
    mates,
    pair_scores,
    uj,
    transit,
    uj_wide,
    uj_tall,
    weights,
    acc,
    sums,
    inverse,
    inverse_own,
    inverse_rows,
    inverse_cols,
    across,
    wide,
    pull_first,
    pull_out,
    pull_in,
    pull_own,
    shares,
    local_sem,
    z_send,
    z_recv,
    near_send,
    near_recv,
    x_send,
    x_recv,
    row_send,
    row_recv,
    sums_send,
    sums_recv,
    inv_send,
    inv_recv,
    sib_send,
    sib_recv,
    share_send,
    share_recv,
    grad_send,
    grad_recv,
):
    blk = lax.axis_index("blk")
    y = lax.axis_index("rep")
    core = lax.rem(blk, CORES)
    x = lax.rem(lax.div(blk, CORES), XS)
    z = lax.div(blk, CORES * XS)
    odd = lax.rem(z, 2)
    z_pair = z + 1 - 2 * odd

    def device(dx=0, dy=0, to_z=None, dc=0):
        there = (z if to_z is None else to_z) * XS + lax.rem(x + (dx % XS), XS)
        return (there * CORES + lax.rem(core + dc, CORES), lax.rem(y + (dy % YS), YS))

    quarters = [lax.rem(k + YS - y, 4) for k in range(4)]
    z_to = [
        lax.rem(z + ZS + jnp.where(lax.rem(z + k, 2) == 0, k, -k), ZS) for k in range(4)
    ]
    z_from = [lax.rem(z + ZS + jnp.where(odd == 0, -k, k), ZS) for k in range(4)]

    embedding_copy = pltpu.make_async_copy(emb_hbm, emb_ref, local_sem.at[0])
    partner_copy = pltpu.make_async_copy(partner_hbm, partner_ref, local_sem.at[1])
    embedding_copy.start()
    partner_copy.start()

    group = [
        (dy, db, dc)
        for dy in range(YS)
        for db in range(2)
        for dc in range(CORES)
        if (dy, db, dc) != (0, 0, 0)
    ]
    group.sort(key=lambda to: -(min(to[0], YS - to[0]) + to[1]))
    near = [device(dc=1), device(to_z=z_pair)]
    near += [device(dx=d) for d in (1, 2, 3)] + [device(dy=d) for d in (1, 2, 3)]
    near += [device(to_z=z_from[k]) for k in (1, 2, 3)]
    barrier = pltpu.get_barrier_semaphore()
    for peer in near:
        pl.semaphore_signal(barrier, inc=1, device_id=peer, device_id_type=MESH)
    own_at = (odd * 2 + core) * ROWS
    own_rows = pl.ds(pl.multiple_of(own_at, ROWS), ROWS)
    sib_rows = pl.ds(pl.multiple_of((odd * 2 + 1 - core) * ROWS, ROWS), ROWS)
    pair_rows = pl.ds(pl.multiple_of(((1 - odd) * 2 + core) * ROWS, ROWS), ROWS)
    last_rows = pl.ds(pl.multiple_of(((1 - odd) * 2 + 1 - core) * ROWS, ROWS), ROWS)

    embedding_copy.wait()
    emb = emb_ref[...]
    norm = jnp.sqrt(jnp.sum(emb * emb, axis=1, keepdims=True) + 1e-12)
    unit = emb / norm
    norms[...] = norm
    ui[own_rows, :] = unit
    first = pl.ds(pl.multiple_of(own_at + quarters[0] * QUARTER, QUARTER), QUARTER)
    uj[0:QUARTER, :] = ui[first, :]
    second = pl.ds(pl.multiple_of(own_at + quarters[1] * QUARTER, QUARTER), QUARTER)
    transit[0:QUARTER, :] = ui[second, :]

    pl.semaphore_wait(barrier, len(near))

    sent = []

    def send(src, dst, send_sem, recv_sem, peer):
        copy = pltpu.make_async_remote_copy(
            src_ref=src,
            dst_ref=dst,
            send_sem=send_sem,
            recv_sem=recv_sem,
            device_id=peer,
            device_id_type=MESH,
        )
        copy.start()
        sent.append(copy)

    def settle():
        for copy in sent:
            copy.wait_send()
        sent.clear()

    def arrived(dst, recv_sem):
        pltpu.make_async_remote_copy(
            src_ref=dst,
            dst_ref=dst,
            send_sem=recv_sem,
            recv_sem=recv_sem,
            device_id=device(dc=1),
            device_id_type=MESH,
        ).wait_recv()

    def quarter(k, column):
        return uj.at[pl.ds(PLACE[k] * ROWS + column * QUARTER, QUARTER)]

    def x_spread(k, place):
        for column, dx in ((3, 2), (1, 1), (2, 3)):
            send(
                place(0),
                place(column),
                x_send.at[k, column - 1],
                x_recv.at[k, column - 1],
                device(dx=dx),
            )

    def in_transit(column):
        return transit.at[pl.ds(column * QUARTER, QUARTER)]

    def x_arrived(k, place):
        for column in range(1, XS):
            arrived(place(column), x_recv.at[k, column - 1])

    def pass_on(column):
        if column:
            arrived(in_transit(column), x_recv.at[1, column - 1])
        send(
            in_transit(column),
            quarter(1, column),
            near_send.at[column],
            near_recv.at[column],
            device(to_z=z_to[1]),
        )

    for k in (3, 2):
        at = pl.ds(pl.multiple_of(own_at + quarters[k] * QUARTER, QUARTER), QUARTER)
        send(ui.at[at], quarter(k, 0), z_send.at[k - 1], z_recv.at[k - 1], device(to_z=z_to[k]))
    x_spread(1, in_transit)
    pass_on(0)
    x_spread(0, functools.partial(quarter, 0))
    rows_of = ui.at[own_rows]
    send(rows_of, rows_of, row_send.at[0], row_recv.at[0], device(dc=1))
    near_rows = ui.at[pl.ds(pl.multiple_of(own_at + y * QUARTER, QUARTER), QUARTER)]
    send(near_rows, near_rows, row_send.at[1], row_recv.at[1], device(to_z=z_pair))
    partner_copy.wait()
    unit = ui[own_rows, :]
    node = lax.broadcasted_iota(jnp.int32, (ROWS, ROWS), 0)
    pairing = (node + blk * ROWS == partner_ref[...]).astype(F32)
    mate = dot_nn(pairing, unit, HIGHEST)
    mates[...] = mate
    pair_scores[...] = dot_nt(jnp.ones((8, WIDTH), F32), unit * mate, HIGHEST)[0:1]
    def take(k):
        arrived(quarter(k, 0), z_recv.at[k - 1])
        x_spread(k, functools.partial(quarter, k))

    def pair_quarter(dy):
        at = ((1 - odd) * 2 + core) * ROWS + lax.rem(y + dy, YS) * QUARTER
        return ui.at[pl.ds(pl.multiple_of(at, QUARTER), QUARTER)]

    def hand_on():
        arrived(pair_quarter(0), row_recv.at[1])
        for dy in (2, 1, 3):
            send(
                pair_quarter(0),
                pair_quarter(0),
                row_send.at[2 + dy],
                row_recv.at[2 + dy],
                device(dy=dy),
            )

    def swap_rows():
        for dy in (1, 2, 3):
            arrived(pair_quarter(YS - dy), row_recv.at[2 + dy])
        rows_of = ui.at[pair_rows]
        send(rows_of, rows_of, row_send.at[2], row_recv.at[2], device(dc=1))

    hand_on()
    pass_on(1)
    pass_on(2)
    take(2)
    take(3)
    pass_on(3)
    swap_rows()
    arrived(ui.at[sib_rows], row_recv.at[0])

    def columns_in(start, stop):
        high, low = split(uj[start:stop, :])
        for i, value in enumerate((high, high, low)):
            uj_wide[start:stop, i * WIDTH : (i + 1) * WIDTH] = value
            half = ALL // 2
            at = i * half + start % half
            uj_tall[start // half, at : at + stop - start, :] = value

    def scores(start, stop, b):
        rows = pl.ds(pl.multiple_of(b * 2 * ROWS, 2 * ROWS), 2 * ROWS)
        score = dot_nt(ui_wide[rows, :], uj_wide[start:stop, :])
        weight = jnp.exp2(score * EXP_SCALE - EXP_SCALE)
        if start == 0:
            col = lax.broadcasted_iota(jnp.int32, (1, stop), 1)
            first_row = own_at - b * 2 * ROWS + quarters[0] * QUARTER
            diagonal = jnp.where(col < QUARTER, col + first_row, 4 * ALL)
            row = lax.broadcasted_iota(jnp.int32, weight.shape, 0)
            weight = jnp.where(row == diagonal, 0.0, weight)
        weights[rows, start:stop] = weight
        tiles = [weight[:, i : i + TILE] for i in range(0, stop - start, TILE)]
        part = tiles[0]
        for tile in tiles[1:]:
            part = part + tile
        if start == 0:
            acc[rows, :] = part
        else:
            acc[rows, :] += part

    def rows_in(b):
        rows = pl.ds(pl.multiple_of(b * 2 * ROWS, 2 * ROWS), 2 * ROWS)
        high, low = split(ui[rows, :])
        for i, value in enumerate((high, low, high)):
            ui_wide[rows, i * WIDTH : (i + 1) * WIDTH] = value

    rows_in(odd)
    x_arrived(0, functools.partial(quarter, 0))
    x_arrived(2, functools.partial(quarter, 2))
    columns_in(0, 384)
    scores(0, 384, odd)
    arrived(ui.at[last_rows], row_recv.at[2])
    rows_in(1 - odd)
    scores(0, 384, 1 - odd)
    for column in range(XS):
        arrived(quarter(1, column), near_recv.at[column])
    columns_in(384, 512)
    for b in (odd, 1 - odd):
        scores(384, 512, b)
    x_arrived(3, functools.partial(quarter, 3))
    columns_in(512, 768)
    for b in (odd, 1 - odd):
        scores(512, 768, b)

    gather_sent = list(sent)
    sent.clear()
    mine = (y * 2 + odd) * CORES + core
    ones = jnp.ones((8, TILE), BF16)
    for i in range(4):
        high, low = split(acc[i * ROWS : (i + 1) * ROWS, :])
        sums[mine, i] = (dot_nt(ones, high) + dot_nt(ones, low))[0:1]
    for i, (dy, db, dc) in enumerate(group):
        send(
            sums.at[mine],
            sums.at[mine],
            sums_send.at[i],
            sums_recv.at[mine],
            device(dy=dy, to_z=z_pair if db else z, dc=dc),
        )
    sums_sent = list(sent)
    sent[:] = gather_sent
    settle()
    for dy, db, dc in group:
        other_b = 1 - odd if db else odd
        other = (lax.rem(y + dy, YS) * 2 + other_b) * CORES + lax.rem(core + dc, CORES)
        arrived(sums.at[other], sums_recv.at[other])
    total = sums[0]
    for i in range(1, 4 * YS):
        total = total + sums[i]
    inverse[...] = 1.0 / total

    own_inverse = inverse[odd * 2 + core]
    for i in range(4):
        inverse_own[i] = own_inverse[:, i * QUARTER : (i + 1) * QUARTER]

    for k in (3, 2, 1, 0):
        for column, dx in ((3, 2), (1, 1), (2, 3), (0, 0)):
            if (k, column) != (0, 0):
                send(
                    inverse_own.at[quarters[k]],
                    inverse_cols.at[k, column],
                    inv_send.at[k, column],
                    inv_recv.at[k, column],
                    device(dx=dx, to_z=z_to[k]),
                )
    inverse_cols[0, 0] = inverse_own[quarters[0]]
    loss_ref[...] = INV_TEMP - jnp.log(own_inverse) - INV_TEMP * pair_scores[...]
    same = lax.broadcasted_iota(jnp.int32, (ROWS, ROWS), 1) == node
    for i in range(4):
        column_sum = jnp.sum(jnp.where(same, inverse[i], 0.0), axis=1, keepdims=True)
        inverse_rows[i * ROWS : (i + 1) * ROWS, :] = jnp.broadcast_to(column_sum, (ROWS, TILE))
    inverse_sent = list(sent)
    sent[:] = sums_sent
    settle()
    def take_inverse(part):
        columns = slice(part * ALL // 2, (part + 1) * ALL // 2)
        pieces = []
        for k in PLACE[2 * part : 2 * part + 2]:
            for column in range(XS):
                if (k, column) != (0, 0):
                    arrived(inverse_cols.at[k, column], inv_recv.at[k, column])
                pieces.append((k, column))
        across[:, columns] = jnp.concatenate([inverse_cols[piece] for piece in pieces], axis=1)

    def pulls(slot, block, part):
        rows = pl.ds(pl.multiple_of(block * ROWS, ROWS), ROWS)
        size = ALL // 2
        for start in range(0, size, TILE):
            tile = slice(part * size + start, part * size + start + TILE)
            both = weights[rows, tile] * (inverse_rows[rows, :] + across[:, tile])
            high, low = split(both)
            for i, value in enumerate((high, low, high)):
                wide[slot, :, i * size + start : i * size + start + TILE] = value
        return dot_nn(wide[slot], uj_tall[part])

    there = (1 - odd, odd)
    blocks = [b * 2 + 1 - core for b in there] + [b * 2 + core for b in there]
    take_inverse(0)
    for i, block in enumerate(blocks):
        pull_first[i] = pulls(i, block, 0)
    take_inverse(1)

    for i in range(2):
        pull_out[i] = pull_first[i] + pulls(i, blocks[i], 1)
        send(pull_out.at[i], pull_in.at[i], sib_send.at[i], sib_recv.at[i], device(dc=1))
    for i in range(2):
        pull_own[i] = pull_first[2 + i] + pulls(2 + i, blocks[2 + i], 1)

    def share(at):
        return pl.ds(pl.multiple_of(at * SHARE, SHARE), SHARE)

    for i in range(2):
        arrived(pull_in.at[i], sib_recv.at[i])
        pull_own[i] += pull_in[i]
        for dy in (2, 1, 3) if i else (2, 1, 3, 0):
            slot = dy - 1 if i else dy + 3
            send(
                pull_own.at[i, share(lax.rem(y + dy, YS))],
                shares.at[slot],
                share_send.at[slot],
                share_recv.at[slot],
                device(dy=dy, to_z=z if i else z_pair),
            )
    shares_sent = list(sent)
    sent[:] = inverse_sent
    settle()
    for slot in range(7):
        arrived(shares.at[slot], share_recv.at[slot])
    rows = pl.ds(pl.multiple_of(y * SHARE, SHARE), SHARE)
    pull = pull_own[1, share(y), :]
    for slot in range(7):
        pull = pull + shares[slot]
    unit = ui[pl.ds(pl.multiple_of(own_at + y * SHARE, SHARE), SHARE), :]
    grad_unit = INV_TEMP * (pull - 2.0 * mates[rows, :])
    along = jnp.sum(unit * grad_unit, axis=1, keepdims=True)
    grad_ref[rows, :] = (grad_unit - unit * along) / norms[rows, :]
    for dy in (2, 1, 3):
        send(
            grad_ref.at[rows],
            grad_ref.at[rows],
            grad_send.at[dy - 1],
            grad_recv.at[dy - 1],
            device(dy=dy),
        )
    sent.extend(shares_sent)
    settle()
    for dy in range(1, YS):
        from_rows = pl.ds(pl.multiple_of(lax.rem(y + YS - dy, YS) * SHARE, SHARE), SHARE)
        arrived(grad_ref.at[from_rows], grad_recv.at[dy - 1])
    settle()


def body(embeddings, partner):
    vmem = pl.BlockSpec(memory_space=pltpu.VMEM)
    hbm = pl.BlockSpec(memory_space=pltpu.HBM)
    dma = pltpu.SemaphoreType.DMA
    loss, grad = pl.pallas_call(
        kernel,
        out_shape=(
            jax.ShapeDtypeStruct((1, ROWS), F32),
            jax.ShapeDtypeStruct((ROWS, WIDTH), F32),
        ),
        in_specs=[hbm, hbm],
        out_specs=(vmem, vmem),
        scratch_shapes=[
            pltpu.VMEM((ROWS, WIDTH), F32),
            pltpu.VMEM((1, ROWS), jnp.int32),
            pltpu.VMEM((ALL, WIDTH), F32),
            pltpu.VMEM((ALL, 3 * WIDTH), BF16),
            pltpu.VMEM((ROWS, 1), F32),
            pltpu.VMEM((ROWS, WIDTH), F32),
            pltpu.VMEM((1, ROWS), F32),
            pltpu.VMEM((ALL, WIDTH), F32),
            pltpu.VMEM((ROWS, WIDTH), F32),
            pltpu.VMEM((ALL, 3 * WIDTH), BF16),
            pltpu.VMEM((2, 3 * ALL // 2, WIDTH), BF16),
            pltpu.VMEM((ALL, ALL), F32),
            pltpu.VMEM((ALL, TILE), F32),
            pltpu.VMEM((4 * YS, 4, 1, ROWS), F32),
            pltpu.VMEM((4, 1, ROWS), F32),
            pltpu.VMEM((4, 1, QUARTER), F32),
            pltpu.VMEM((ALL, TILE), F32),
            pltpu.VMEM((4, XS, 1, QUARTER), F32),
            pltpu.VMEM((1, ALL), F32),
            pltpu.VMEM((4, ROWS, 3 * ALL // 2), BF16),
            pltpu.VMEM((4, ROWS, WIDTH), F32),
            pltpu.VMEM((2, ROWS, WIDTH), F32),
            pltpu.VMEM((2, ROWS, WIDTH), F32),
            pltpu.VMEM((2, ROWS, WIDTH), F32),
            pltpu.VMEM((7, SHARE, WIDTH), F32),
            dma((2,)),
            dma((3,)),
            dma((3,)),
            dma((4,)),
            dma((4,)),
            dma((4, 3)),
            dma((4, 3)),
            dma((6,)),
            dma((6,)),
            dma((15,)),
            dma((16,)),
            dma((4, 4)),
            dma((4, 4)),
            dma((2,)),
            dma((2,)),
            dma((7,)),
            dma((7,)),
            dma((3,)),
            dma((3,)),
        ],
        compiler_params=pltpu.CompilerParams(
            collective_id=0, has_side_effects=True, vmem_limit_bytes=56254464
        ),
    )(embeddings, partner.reshape(1, ROWS))
    def write(loss_vmem, grad_vmem, loss_out, grad_out, sems):
        copies = [
            pltpu.make_async_copy(grad_vmem, grad_out, sems.at[0]),
            pltpu.make_async_copy(loss_vmem, loss_out, sems.at[1]),
        ]
        for copy in copies:
            copy.start()
        for copy in copies:
            copy.wait()

    loss, grad = pl.pallas_call(
        write,
        out_shape=(
            jax.ShapeDtypeStruct((1, ROWS), F32),
            jax.ShapeDtypeStruct((ROWS, WIDTH), F32),
        ),
        in_specs=[pl.BlockSpec(memory_space=pl.ANY)] * 2,
        out_specs=(hbm, hbm),
        scratch_shapes=[dma((2,))],
        compiler_params=pltpu.CompilerParams(vmem_limit_bytes=2**20),
    )(loss, grad)
    return loss.reshape(ROWS), grad


def solution(mesh):
    return jax.shard_map(
        body,
        mesh=mesh,
        in_specs=(P("blk", None), P("blk")),
        out_specs=(P("blk"), P("blk", None)),
        check_vma=False,
    )
```

```python
import functools
import math

import jax
import jax.numpy as jnp
from jax import lax
from jax.experimental import pallas as pl
from jax.experimental.pallas import tpu as pltpu
from jax.sharding import PartitionSpec as P

MESH = pl.DeviceIdType.MESH
F32 = jnp.float32
BF16 = jnp.bfloat16
HIGHEST = lax.Precision.HIGHEST
INV_TEMP = 10.0
EXP_SCALE = INV_TEMP * math.log2(math.e)
ROWS = 192
WIDTH = 256
XS, YS, ZS, CORES = 4, 4, 8, 2
QUARTER = ROWS // 4
SHARE = ROWS // YS
TILE = 128
PLACE = (0, 2, 1, 3)
ALL = 4 * ROWS


def dot_nn(a, b, precision=None):
    return lax.dot_general(
        a, b, (((1,), (0,)), ((), ())), precision=precision, preferred_element_type=F32
    )


def dot_nt(a, b, precision=None):
    return lax.dot_general(
        a, b, (((1,), (1,)), ((), ())), precision=precision, preferred_element_type=F32
    )


def split(value):
    high = value.astype(BF16)
    return high, (value - high.astype(F32)).astype(BF16)


def kernel(
    emb_hbm,
    partner_hbm,
    loss_ref,
    grad_ref,
    emb_ref,
    partner_ref,
    ui,
    ui_wide,
    norms,
    mates,
    pair_scores,
    uj,
    transit,
    uj_wide,
    uj_tall,
    weights,
    acc,
    sums,
    inverse,
    inverse_own,
    inverse_rows,
    inverse_cols,
    across,
    wide,
    pull_first,
    pull_out,
    pull_in,
    pull_own,
    shares,
    local_sem,
    z_send,
    z_recv,
    near_send,
    near_recv,
    x_send,
    x_recv,
    row_send,
    row_recv,
    sums_send,
    sums_recv,
    inv_send,
    inv_recv,
    sib_send,
    sib_recv,
    share_send,
    share_recv,
    grad_send,
    grad_recv,
):
    blk = lax.axis_index("blk")
    y = lax.axis_index("rep")
    core = lax.rem(blk, CORES)
    x = lax.rem(lax.div(blk, CORES), XS)
    z = lax.div(blk, CORES * XS)
    odd = lax.rem(z, 2)
    z_pair = z + 1 - 2 * odd

    def device(dx=0, dy=0, to_z=None, dc=0):
        there = (z if to_z is None else to_z) * XS + lax.rem(x + (dx % XS), XS)
        return (there * CORES + lax.rem(core + dc, CORES), lax.rem(y + (dy % YS), YS))

    quarters = [lax.rem(k + YS - y, 4) for k in range(4)]
    z_to = [
        lax.rem(z + ZS + jnp.where(lax.rem(z + k, 2) == 0, k, -k), ZS) for k in range(4)
    ]
    z_from = [lax.rem(z + ZS + jnp.where(odd == 0, -k, k), ZS) for k in range(4)]

    embedding_copy = pltpu.make_async_copy(emb_hbm, emb_ref, local_sem.at[0])
    partner_copy = pltpu.make_async_copy(partner_hbm, partner_ref, local_sem.at[1])
    embedding_copy.start()
    partner_copy.start()

    group = [
        (dy, db, dc)
        for dy in range(YS)
        for db in range(2)
        for dc in range(CORES)
        if (dy, db, dc) != (0, 0, 0)
    ]
    group.sort(key=lambda to: -(min(to[0], YS - to[0]) + to[1]))
    near = [device(dc=1), device(to_z=z_pair)]
    near += [device(dx=d) for d in (1, 2, 3)] + [device(dy=d) for d in (1, 2, 3)]
    near += [device(to_z=z_from[k]) for k in (1, 2, 3)]
    barrier = pltpu.get_barrier_semaphore()
    for peer in near:
        pl.semaphore_signal(barrier, inc=1, device_id=peer, device_id_type=MESH)
    own_at = (odd * 2 + core) * ROWS
    own_rows = pl.ds(pl.multiple_of(own_at, ROWS), ROWS)
    sib_rows = pl.ds(pl.multiple_of((odd * 2 + 1 - core) * ROWS, ROWS), ROWS)
    pair_rows = pl.ds(pl.multiple_of(((1 - odd) * 2 + core) * ROWS, ROWS), ROWS)
    last_rows = pl.ds(pl.multiple_of(((1 - odd) * 2 + 1 - core) * ROWS, ROWS), ROWS)

    embedding_copy.wait()
    emb = emb_ref[...]
    norm = jnp.sqrt(jnp.sum(emb * emb, axis=1, keepdims=True) + 1e-12)
    unit = emb / norm
    norms[...] = norm
    ui[own_rows, :] = unit
    first = pl.ds(pl.multiple_of(own_at + quarters[0] * QUARTER, QUARTER), QUARTER)
    uj[0:QUARTER, :] = ui[first, :]
    second = pl.ds(pl.multiple_of(own_at + quarters[1] * QUARTER, QUARTER), QUARTER)
    transit[0:QUARTER, :] = ui[second, :]

    pl.semaphore_wait(barrier, len(near))

    sent = []

    def send(src, dst, send_sem, recv_sem, peer):
        copy = pltpu.make_async_remote_copy(
            src_ref=src,
            dst_ref=dst,
            send_sem=send_sem,
            recv_sem=recv_sem,
            device_id=peer,
            device_id_type=MESH,
        )
        copy.start()
        sent.append(copy)

    def settle():
        for copy in sent:
            copy.wait_send()
        sent.clear()

    def arrived(dst, recv_sem):
        pltpu.make_async_remote_copy(
            src_ref=dst,
            dst_ref=dst,
            send_sem=recv_sem,
            recv_sem=recv_sem,
            device_id=device(dc=1),
            device_id_type=MESH,
        ).wait_recv()

    def quarter(k, column):
        return uj.at[pl.ds(PLACE[k] * ROWS + column * QUARTER, QUARTER)]

    def x_spread(k, place):
        for column, dx in ((3, 2), (1, 1), (2, 3)):
            send(
                place(0),
                place(column),
                x_send.at[k, column - 1],
                x_recv.at[k, column - 1],
                device(dx=dx),
            )

    def in_transit(column):
        return transit.at[pl.ds(column * QUARTER, QUARTER)]

    def x_arrived(k, place):
        for column in range(1, XS):
            arrived(place(column), x_recv.at[k, column - 1])

    def pass_on(column):
        if column:
            arrived(in_transit(column), x_recv.at[1, column - 1])
        send(
            in_transit(column),
            quarter(1, column),
            near_send.at[column],
            near_recv.at[column],
            device(to_z=z_to[1]),
        )

    for k in (2, 3):
        at = pl.ds(pl.multiple_of(own_at + quarters[k] * QUARTER, QUARTER), QUARTER)
        send(ui.at[at], quarter(k, 0), z_send.at[k - 1], z_recv.at[k - 1], device(to_z=z_to[k]))
    x_spread(1, in_transit)
    pass_on(0)
    x_spread(0, functools.partial(quarter, 0))
    rows_of = ui.at[own_rows]
    send(rows_of, rows_of, row_send.at[0], row_recv.at[0], device(dc=1))
    near_rows = ui.at[pl.ds(pl.multiple_of(own_at + y * QUARTER, QUARTER), QUARTER)]
    send(near_rows, near_rows, row_send.at[1], row_recv.at[1], device(to_z=z_pair))
    partner_copy.wait()
    unit = ui[own_rows, :]
    node = lax.broadcasted_iota(jnp.int32, (ROWS, ROWS), 0)
    pairing = (node + blk * ROWS == partner_ref[...]).astype(F32)
    mate = dot_nn(pairing, unit, HIGHEST)
    mates[...] = mate
    pair_scores[...] = dot_nt(jnp.ones((8, WIDTH), F32), unit * mate, HIGHEST)[0:1]
    def take(k):
        arrived(quarter(k, 0), z_recv.at[k - 1])
        x_spread(k, functools.partial(quarter, k))

    def pair_quarter(dy):
        at = ((1 - odd) * 2 + core) * ROWS + lax.rem(y + dy, YS) * QUARTER
        return ui.at[pl.ds(pl.multiple_of(at, QUARTER), QUARTER)]

    def hand_on():
        arrived(pair_quarter(0), row_recv.at[1])
        for dy in (2, 1, 3):
            send(
                pair_quarter(0),
                pair_quarter(0),
                row_send.at[2 + dy],
                row_recv.at[2 + dy],
                device(dy=dy),
            )

    def swap_rows():
        for dy in (1, 2, 3):
            arrived(pair_quarter(YS - dy), row_recv.at[2 + dy])
        rows_of = ui.at[pair_rows]
        send(rows_of, rows_of, row_send.at[2], row_recv.at[2], device(dc=1))

    hand_on()
    pass_on(1)
    pass_on(2)
    take(2)
    take(3)
    pass_on(3)
    swap_rows()
    arrived(ui.at[sib_rows], row_recv.at[0])

    def columns_in(start, stop):
        high, low = split(uj[start:stop, :])
        for i, value in enumerate((high, high, low)):
            uj_wide[start:stop, i * WIDTH : (i + 1) * WIDTH] = value
            half = ALL // 2
            at = i * half + start % half
            uj_tall[start // half, at : at + stop - start, :] = value

    def scores(start, stop, b):
        rows = pl.ds(pl.multiple_of(b * 2 * ROWS, 2 * ROWS), 2 * ROWS)
        score = dot_nt(ui_wide[rows, :], uj_wide[start:stop, :])
        weight = jnp.exp2(score * EXP_SCALE - EXP_SCALE)
        if start == 0:
            col = lax.broadcasted_iota(jnp.int32, (1, stop), 1)
            first_row = own_at - b * 2 * ROWS + quarters[0] * QUARTER
            diagonal = jnp.where(col < QUARTER, col + first_row, 4 * ALL)
            row = lax.broadcasted_iota(jnp.int32, weight.shape, 0)
            weight = jnp.where(row == diagonal, 0.0, weight)
        weights[rows, start:stop] = weight
        tiles = [weight[:, i : i + TILE] for i in range(0, stop - start, TILE)]
        part = tiles[0]
        for tile in tiles[1:]:
            part = part + tile
        if start == 0:
            acc[rows, :] = part
        else:
            acc[rows, :] += part

    def rows_in(b):
        rows = pl.ds(pl.multiple_of(b * 2 * ROWS, 2 * ROWS), 2 * ROWS)
        high, low = split(ui[rows, :])
        for i, value in enumerate((high, low, high)):
            ui_wide[rows, i * WIDTH : (i + 1) * WIDTH] = value

    rows_in(odd)
    x_arrived(0, functools.partial(quarter, 0))
    x_arrived(2, functools.partial(quarter, 2))
    columns_in(0, 384)
    scores(0, 384, odd)
    arrived(ui.at[last_rows], row_recv.at[2])
    rows_in(1 - odd)
    scores(0, 384, 1 - odd)
    for column in range(XS):
        arrived(quarter(1, column), near_recv.at[column])
    columns_in(384, 512)
    for b in (odd, 1 - odd):
        scores(384, 512, b)
    x_arrived(3, functools.partial(quarter, 3))
    columns_in(512, 768)
    for b in (odd, 1 - odd):
        scores(512, 768, b)

    gather_sent = list(sent)
    sent.clear()
    mine = (y * 2 + odd) * CORES + core
    ones = jnp.ones((8, TILE), BF16)
    for i in range(4):
        high, low = split(acc[i * ROWS : (i + 1) * ROWS, :])
        sums[mine, i] = (dot_nt(ones, high) + dot_nt(ones, low))[0:1]
    for i, (dy, db, dc) in enumerate(group):
        send(
            sums.at[mine],
            sums.at[mine],
            sums_send.at[i],
            sums_recv.at[mine],
            device(dy=dy, to_z=z_pair if db else z, dc=dc),
        )
    sums_sent = list(sent)
    sent[:] = gather_sent
    settle()
    for dy, db, dc in group:
        other_b = 1 - odd if db else odd
        other = (lax.rem(y + dy, YS) * 2 + other_b) * CORES + lax.rem(core + dc, CORES)
        arrived(sums.at[other], sums_recv.at[other])
    total = sums[0]
    for i in range(1, 4 * YS):
        total = total + sums[i]
    inverse[...] = 1.0 / total

    own_inverse = inverse[odd * 2 + core]
    for i in range(4):
        inverse_own[i] = own_inverse[:, i * QUARTER : (i + 1) * QUARTER]

    for k in (3, 2, 1, 0):
        for column, dx in ((3, 2), (1, 1), (2, 3), (0, 0)):
            if (k, column) != (0, 0):
                send(
                    inverse_own.at[quarters[k]],
                    inverse_cols.at[k, column],
                    inv_send.at[k, column],
                    inv_recv.at[k, column],
                    device(dx=dx, to_z=z_to[k]),
                )
    inverse_cols[0, 0] = inverse_own[quarters[0]]
    loss_ref[...] = INV_TEMP - jnp.log(own_inverse) - INV_TEMP * pair_scores[...]
    same = lax.broadcasted_iota(jnp.int32, (ROWS, ROWS), 1) == node
    for i in range(4):
        column_sum = jnp.sum(jnp.where(same, inverse[i], 0.0), axis=1, keepdims=True)
        inverse_rows[i * ROWS : (i + 1) * ROWS, :] = jnp.broadcast_to(column_sum, (ROWS, TILE))
    inverse_sent = list(sent)
    sent[:] = sums_sent
    settle()
    def take_inverse(part):
        columns = slice(part * ALL // 2, (part + 1) * ALL // 2)
        pieces = []
        for k in PLACE[2 * part : 2 * part + 2]:
            for column in range(XS):
                if (k, column) != (0, 0):
                    arrived(inverse_cols.at[k, column], inv_recv.at[k, column])
                pieces.append((k, column))
        across[:, columns] = jnp.concatenate([inverse_cols[piece] for piece in pieces], axis=1)

    def pulls(slot, block, part):
        rows = pl.ds(pl.multiple_of(block * ROWS, ROWS), ROWS)
        size = ALL // 2
        for start in range(0, size, TILE):
            tile = slice(part * size + start, part * size + start + TILE)
            both = weights[rows, tile] * (inverse_rows[rows, :] + across[:, tile])
            high, low = split(both)
            for i, value in enumerate((high, low, high)):
                wide[slot, :, i * size + start : i * size + start + TILE] = value
        return dot_nn(wide[slot], uj_tall[part])

    there = (1 - odd, odd)
    blocks = [b * 2 + 1 - core for b in there] + [b * 2 + core for b in there]
    take_inverse(0)
    for i, block in enumerate(blocks):
        pull_first[i] = pulls(i, block, 0)
    take_inverse(1)

    for i in range(2):
        pull_out[i] = pull_first[i] + pulls(i, blocks[i], 1)
        send(pull_out.at[i], pull_in.at[i], sib_send.at[i], sib_recv.at[i], device(dc=1))
        pull_own[i] = pull_first[2 + i] + pulls(2 + i, blocks[2 + i], 1)

    def share(at):
        return pl.ds(pl.multiple_of(at * SHARE, SHARE), SHARE)

    for i in range(2):
        arrived(pull_in.at[i], sib_recv.at[i])
        pull_own[i] += pull_in[i]
        for dy in (2, 1, 3) if i else (2, 1, 3, 0):
            slot = dy - 1 if i else dy + 3
            send(
                pull_own.at[i, share(lax.rem(y + dy, YS))],
                shares.at[slot],
                share_send.at[slot],
                share_recv.at[slot],
                device(dy=dy, to_z=z if i else z_pair),
            )
    shares_sent = list(sent)
    sent[:] = inverse_sent
    settle()
    for slot in range(7):
        arrived(shares.at[slot], share_recv.at[slot])
    rows = pl.ds(pl.multiple_of(y * SHARE, SHARE), SHARE)
    pull = pull_own[1, share(y), :]
    for slot in range(7):
        pull = pull + shares[slot]
    unit = ui[pl.ds(pl.multiple_of(own_at + y * SHARE, SHARE), SHARE), :]
    grad_unit = INV_TEMP * (pull - 2.0 * mates[rows, :])
    along = jnp.sum(unit * grad_unit, axis=1, keepdims=True)
    grad_ref[rows, :] = (grad_unit - unit * along) / norms[rows, :]
    for dy in (2, 1, 3):
        send(
            grad_ref.at[rows],
            grad_ref.at[rows],
            grad_send.at[dy - 1],
            grad_recv.at[dy - 1],
            device(dy=dy),
        )
    sent.extend(shares_sent)
    settle()
    for dy in range(1, YS):
        from_rows = pl.ds(pl.multiple_of(lax.rem(y + YS - dy, YS) * SHARE, SHARE), SHARE)
        arrived(grad_ref.at[from_rows], grad_recv.at[dy - 1])
    settle()


def body(embeddings, partner):
    vmem = pl.BlockSpec(memory_space=pltpu.VMEM)
    hbm = pl.BlockSpec(memory_space=pltpu.HBM)
    dma = pltpu.SemaphoreType.DMA
    loss, grad = pl.pallas_call(
        kernel,
        out_shape=(
            jax.ShapeDtypeStruct((1, ROWS), F32),
            jax.ShapeDtypeStruct((ROWS, WIDTH), F32),
        ),
        in_specs=[hbm, hbm],
        out_specs=(vmem, vmem),
        scratch_shapes=[
            pltpu.VMEM((ROWS, WIDTH), F32),
            pltpu.VMEM((1, ROWS), jnp.int32),
            pltpu.VMEM((ALL, WIDTH), F32),
            pltpu.VMEM((ALL, 3 * WIDTH), BF16),
            pltpu.VMEM((ROWS, 1), F32),
            pltpu.VMEM((ROWS, WIDTH), F32),
            pltpu.VMEM((1, ROWS), F32),
            pltpu.VMEM((ALL, WIDTH), F32),
            pltpu.VMEM((ROWS, WIDTH), F32),
            pltpu.VMEM((ALL, 3 * WIDTH), BF16),
            pltpu.VMEM((2, 3 * ALL // 2, WIDTH), BF16),
            pltpu.VMEM((ALL, ALL), F32),
            pltpu.VMEM((ALL, TILE), F32),
            pltpu.VMEM((4 * YS, 4, 1, ROWS), F32),
            pltpu.VMEM((4, 1, ROWS), F32),
            pltpu.VMEM((4, 1, QUARTER), F32),
            pltpu.VMEM((ALL, TILE), F32),
            pltpu.VMEM((4, XS, 1, QUARTER), F32),
            pltpu.VMEM((1, ALL), F32),
            pltpu.VMEM((4, ROWS, 3 * ALL // 2), BF16),
            pltpu.VMEM((4, ROWS, WIDTH), F32),
            pltpu.VMEM((2, ROWS, WIDTH), F32),
            pltpu.VMEM((2, ROWS, WIDTH), F32),
            pltpu.VMEM((2, ROWS, WIDTH), F32),
            pltpu.VMEM((7, SHARE, WIDTH), F32),
            dma((2,)),
            dma((3,)),
            dma((3,)),
            dma((4,)),
            dma((4,)),
            dma((4, 3)),
            dma((4, 3)),
            dma((6,)),
            dma((6,)),
            dma((15,)),
            dma((16,)),
            dma((4, 4)),
            dma((4, 4)),
            dma((2,)),
            dma((2,)),
            dma((7,)),
            dma((7,)),
            dma((3,)),
            dma((3,)),
        ],
        compiler_params=pltpu.CompilerParams(
            collective_id=0, has_side_effects=True, vmem_limit_bytes=56254464
        ),
    )(embeddings, partner.reshape(1, ROWS))
    def write(loss_vmem, grad_vmem, loss_out, grad_out, sems):
        copies = [
            pltpu.make_async_copy(grad_vmem, grad_out, sems.at[0]),
            pltpu.make_async_copy(loss_vmem, loss_out, sems.at[1]),
        ]
        for copy in copies:
            copy.start()
        for copy in copies:
            copy.wait()

    loss, grad = pl.pallas_call(
        write,
        out_shape=(
            jax.ShapeDtypeStruct((1, ROWS), F32),
            jax.ShapeDtypeStruct((ROWS, WIDTH), F32),
        ),
        in_specs=[pl.BlockSpec(memory_space=pl.ANY)] * 2,
        out_specs=(hbm, hbm),
        scratch_shapes=[dma((2,))],
        compiler_params=pltpu.CompilerParams(vmem_limit_bytes=2**20),
    )(loss, grad)
    return loss.reshape(ROWS), grad


def solution(mesh):
    return jax.shard_map(
        body,
        mesh=mesh,
        in_specs=(P("blk", None), P("blk")),
        out_specs=(P("blk"), P("blk", None)),
        check_vma=False,
    )
```

```python
import functools
import math

import jax
import jax.numpy as jnp
from jax import lax
from jax.experimental import pallas as pl
from jax.experimental.pallas import tpu as pltpu
from jax.sharding import PartitionSpec as P

MESH = pl.DeviceIdType.MESH
F32 = jnp.float32
BF16 = jnp.bfloat16
HIGHEST = lax.Precision.HIGHEST
INV_TEMP = 10.0
EXP_SCALE = INV_TEMP * math.log2(math.e)
ROWS = 192
WIDTH = 256
XS, YS, ZS, CORES = 4, 4, 8, 2
QUARTER = ROWS // 4
SHARE = ROWS // YS
TILE = 128
PLACE = (0, 2, 1, 3)
ALL = 4 * ROWS


def dot_nn(a, b, precision=None):
    return lax.dot_general(
        a, b, (((1,), (0,)), ((), ())), precision=precision, preferred_element_type=F32
    )


def dot_nt(a, b, precision=None):
    return lax.dot_general(
        a, b, (((1,), (1,)), ((), ())), precision=precision, preferred_element_type=F32
    )


def split(value):
    high = value.astype(BF16)
    return high, (value - high.astype(F32)).astype(BF16)


def kernel(
    emb_hbm,
    partner_hbm,
    loss_ref,
    grad_ref,
    emb_ref,
    partner_ref,
    ui,
    ui_wide,
    norms,
    mates,
    pair_scores,
    uj,
    transit,
    uj_wide,
    uj_tall,
    weights,
    acc,
    sums,
    inverse,
    inverse_own,
    inverse_rows,
    inverse_cols,
    across,
    wide,
    pull_first,
    pull_out,
    pull_in,
    pull_own,
    shares,
    local_sem,
    z_send,
    z_recv,
    near_send,
    near_recv,
    x_send,
    x_recv,
    row_send,
    row_recv,
    sums_send,
    sums_recv,
    inv_send,
    inv_recv,
    sib_send,
    sib_recv,
    share_send,
    share_recv,
    grad_send,
    grad_recv,
):
    blk = lax.axis_index("blk")
    y = lax.axis_index("rep")
    core = lax.rem(blk, CORES)
    x = lax.rem(lax.div(blk, CORES), XS)
    z = lax.div(blk, CORES * XS)
    odd = lax.rem(z, 2)
    z_pair = z + 1 - 2 * odd

    def device(dx=0, dy=0, to_z=None, dc=0):
        there = (z if to_z is None else to_z) * XS + lax.rem(x + (dx % XS), XS)
        return (there * CORES + lax.rem(core + dc, CORES), lax.rem(y + (dy % YS), YS))

    quarters = [lax.rem(k + YS - y, 4) for k in range(4)]
    z_to = [
        lax.rem(z + ZS + jnp.where(lax.rem(z + k, 2) == 0, k, -k), ZS) for k in range(4)
    ]
    z_from = [lax.rem(z + ZS + jnp.where(odd == 0, -k, k), ZS) for k in range(4)]

    embedding_copy = pltpu.make_async_copy(emb_hbm, emb_ref, local_sem.at[0])
    partner_copy = pltpu.make_async_copy(partner_hbm, partner_ref, local_sem.at[1])
    embedding_copy.start()
    partner_copy.start()

    group = [
        (dy, db, dc)
        for dy in range(YS)
        for db in range(2)
        for dc in range(CORES)
        if (dy, db, dc) != (0, 0, 0)
    ]
    group.sort(key=lambda to: -(min(to[0], YS - to[0]) + to[1]))
    near = [device(dc=1), device(to_z=z_pair)]
    near += [device(dx=d) for d in (1, 2, 3)] + [device(dy=d) for d in (1, 2, 3)]
    near += [device(to_z=z_from[k]) for k in (1, 2, 3)]
    barrier = pltpu.get_barrier_semaphore()
    for peer in near:
        pl.semaphore_signal(barrier, inc=1, device_id=peer, device_id_type=MESH)
    own_at = (odd * 2 + core) * ROWS
    own_rows = pl.ds(pl.multiple_of(own_at, ROWS), ROWS)
    sib_rows = pl.ds(pl.multiple_of((odd * 2 + 1 - core) * ROWS, ROWS), ROWS)
    pair_rows = pl.ds(pl.multiple_of(((1 - odd) * 2 + core) * ROWS, ROWS), ROWS)
    last_rows = pl.ds(pl.multiple_of(((1 - odd) * 2 + 1 - core) * ROWS, ROWS), ROWS)

    embedding_copy.wait()
    emb = emb_ref[...]
    norm = jnp.sqrt(jnp.sum(emb * emb, axis=1, keepdims=True) + 1e-12)
    unit = emb / norm
    norms[...] = norm
    ui[own_rows, :] = unit
    first = pl.ds(pl.multiple_of(own_at + quarters[0] * QUARTER, QUARTER), QUARTER)
    uj[0:QUARTER, :] = ui[first, :]
    second = pl.ds(pl.multiple_of(own_at + quarters[1] * QUARTER, QUARTER), QUARTER)
    transit[0:QUARTER, :] = ui[second, :]

    pl.semaphore_wait(barrier, len(near))

    sent = []

    def send(src, dst, send_sem, recv_sem, peer):
        copy = pltpu.make_async_remote_copy(
            src_ref=src,
            dst_ref=dst,
            send_sem=send_sem,
            recv_sem=recv_sem,
            device_id=peer,
            device_id_type=MESH,
        )
        copy.start()
        sent.append(copy)

    def settle():
        for copy in sent:
            copy.wait_send()
        sent.clear()

    def arrived(dst, recv_sem):
        pltpu.make_async_remote_copy(
            src_ref=dst,
            dst_ref=dst,
            send_sem=recv_sem,
            recv_sem=recv_sem,
            device_id=device(dc=1),
            device_id_type=MESH,
        ).wait_recv()

    def quarter(k, column):
        return uj.at[pl.ds(PLACE[k] * ROWS + column * QUARTER, QUARTER)]

    def x_spread(k, place):
        for column, dx in ((3, 2), (1, 1), (2, 3)):
            send(
                place(0),
                place(column),
                x_send.at[k, column - 1],
                x_recv.at[k, column - 1],
                device(dx=dx),
            )

    def in_transit(column):
        return transit.at[pl.ds(column * QUARTER, QUARTER)]

    def x_arrived(k, place):
        for column in range(1, XS):
            arrived(place(column), x_recv.at[k, column - 1])

    def pass_on(column):
        if column:
            arrived(in_transit(column), x_recv.at[1, column - 1])
        send(
            in_transit(column),
            quarter(1, column),
            near_send.at[column],
            near_recv.at[column],
            device(to_z=z_to[1]),
        )

    for k in (3, 2):
        at = pl.ds(pl.multiple_of(own_at + quarters[k] * QUARTER, QUARTER), QUARTER)
        send(ui.at[at], quarter(k, 0), z_send.at[k - 1], z_recv.at[k - 1], device(to_z=z_to[k]))
    x_spread(1, in_transit)
    pass_on(0)
    x_spread(0, functools.partial(quarter, 0))
    rows_of = ui.at[own_rows]
    send(rows_of, rows_of, row_send.at[0], row_recv.at[0], device(dc=1))
    near_rows = ui.at[pl.ds(pl.multiple_of(own_at + y * QUARTER, QUARTER), QUARTER)]
    send(near_rows, near_rows, row_send.at[1], row_recv.at[1], device(to_z=z_pair))
    partner_copy.wait()
    unit = ui[own_rows, :]
    node = lax.broadcasted_iota(jnp.int32, (ROWS, ROWS), 0)
    pairing = (node + blk * ROWS == partner_ref[...]).astype(F32)
    mate = dot_nn(pairing, unit, HIGHEST)
    mates[...] = mate
    pair_scores[...] = dot_nt(jnp.ones((8, WIDTH), F32), unit * mate, HIGHEST)[0:1]
    def take(k):
        arrived(quarter(k, 0), z_recv.at[k - 1])
        x_spread(k, functools.partial(quarter, k))

    def pair_quarter(dy):
        at = ((1 - odd) * 2 + core) * ROWS + lax.rem(y + dy, YS) * QUARTER
        return ui.at[pl.ds(pl.multiple_of(at, QUARTER), QUARTER)]

    def hand_on():
        arrived(pair_quarter(0), row_recv.at[1])
        for dy in (2, 1, 3):
            send(
                pair_quarter(0),
                pair_quarter(0),
                row_send.at[2 + dy],
                row_recv.at[2 + dy],
                device(dy=dy),
            )

    def swap_rows():
        for dy in (1, 2, 3):
            arrived(pair_quarter(YS - dy), row_recv.at[2 + dy])
        rows_of = ui.at[pair_rows]
        send(rows_of, rows_of, row_send.at[2], row_recv.at[2], device(dc=1))

    hand_on()
    take(2)
    pass_on(1)
    pass_on(2)
    take(3)
    pass_on(3)
    swap_rows()
    arrived(ui.at[sib_rows], row_recv.at[0])

    def columns_in(start, stop):
        high, low = split(uj[start:stop, :])
        for i, value in enumerate((high, high, low)):
            uj_wide[start:stop, i * WIDTH : (i + 1) * WIDTH] = value
            half = ALL // 2
            at = i * half + start % half
            uj_tall[start // half, at : at + stop - start, :] = value

    def scores(start, stop, b):
        rows = pl.ds(pl.multiple_of(b * 2 * ROWS, 2 * ROWS), 2 * ROWS)
        score = dot_nt(ui_wide[rows, :], uj_wide[start:stop, :])
        weight = jnp.exp2(score * EXP_SCALE - EXP_SCALE)
        if start == 0:
            col = lax.broadcasted_iota(jnp.int32, (1, stop), 1)
            first_row = own_at - b * 2 * ROWS + quarters[0] * QUARTER
            diagonal = jnp.where(col < QUARTER, col + first_row, 4 * ALL)
            row = lax.broadcasted_iota(jnp.int32, weight.shape, 0)
            weight = jnp.where(row == diagonal, 0.0, weight)
        weights[rows, start:stop] = weight
        tiles = [weight[:, i : i + TILE] for i in range(0, stop - start, TILE)]
        part = tiles[0]
        for tile in tiles[1:]:
            part = part + tile
        if start == 0:
            acc[rows, :] = part
        else:
            acc[rows, :] += part

    def rows_in(b):
        rows = pl.ds(pl.multiple_of(b * 2 * ROWS, 2 * ROWS), 2 * ROWS)
        high, low = split(ui[rows, :])
        for i, value in enumerate((high, low, high)):
            ui_wide[rows, i * WIDTH : (i + 1) * WIDTH] = value

    rows_in(odd)
    x_arrived(0, functools.partial(quarter, 0))
    x_arrived(2, functools.partial(quarter, 2))
    columns_in(0, 384)
    scores(0, 384, odd)
    arrived(ui.at[last_rows], row_recv.at[2])
    rows_in(1 - odd)
    scores(0, 384, 1 - odd)
    for column in range(XS):
        arrived(quarter(1, column), near_recv.at[column])
    columns_in(384, 512)
    for b in (odd, 1 - odd):
        scores(384, 512, b)
    x_arrived(3, functools.partial(quarter, 3))
    columns_in(512, 768)
    for b in (odd, 1 - odd):
        scores(512, 768, b)

    gather_sent = list(sent)
    sent.clear()
    mine = (y * 2 + odd) * CORES + core
    ones = jnp.ones((8, TILE), BF16)
    for i in range(4):
        high, low = split(acc[i * ROWS : (i + 1) * ROWS, :])
        sums[mine, i] = (dot_nt(ones, high) + dot_nt(ones, low))[0:1]
    for i, (dy, db, dc) in enumerate(group):
        send(
            sums.at[mine],
            sums.at[mine],
            sums_send.at[i],
            sums_recv.at[mine],
            device(dy=dy, to_z=z_pair if db else z, dc=dc),
        )
    sums_sent = list(sent)
    sent[:] = gather_sent
    settle()
    for dy, db, dc in group:
        other_b = 1 - odd if db else odd
        other = (lax.rem(y + dy, YS) * 2 + other_b) * CORES + lax.rem(core + dc, CORES)
        arrived(sums.at[other], sums_recv.at[other])
    total = sums[0]
    for i in range(1, 4 * YS):
        total = total + sums[i]
    inverse[...] = 1.0 / total

    own_inverse = inverse[odd * 2 + core]
    for i in range(4):
        inverse_own[i] = own_inverse[:, i * QUARTER : (i + 1) * QUARTER]

    for k in (3, 2, 1, 0):
        for column, dx in ((3, 2), (1, 1), (2, 3), (0, 0)):
            if (k, column) != (0, 0):
                send(
                    inverse_own.at[quarters[k]],
                    inverse_cols.at[k, column],
                    inv_send.at[k, column],
                    inv_recv.at[k, column],
                    device(dx=dx, to_z=z_to[k]),
                )
    inverse_cols[0, 0] = inverse_own[quarters[0]]
    loss_ref[...] = INV_TEMP - jnp.log(own_inverse) - INV_TEMP * pair_scores[...]
    same = lax.broadcasted_iota(jnp.int32, (ROWS, ROWS), 1) == node
    for i in range(4):
        column_sum = jnp.sum(jnp.where(same, inverse[i], 0.0), axis=1, keepdims=True)
        inverse_rows[i * ROWS : (i + 1) * ROWS, :] = jnp.broadcast_to(column_sum, (ROWS, TILE))
    inverse_sent = list(sent)
    sent[:] = sums_sent
    settle()
    def take_inverse(part):
        columns = slice(part * ALL // 2, (part + 1) * ALL // 2)
        pieces = []
        for k in PLACE[2 * part : 2 * part + 2]:
            for column in range(XS):
                if (k, column) != (0, 0):
                    arrived(inverse_cols.at[k, column], inv_recv.at[k, column])
                pieces.append((k, column))
        across[:, columns] = jnp.concatenate([inverse_cols[piece] for piece in pieces], axis=1)

    def pulls(slot, block, part):
        rows = pl.ds(pl.multiple_of(block * ROWS, ROWS), ROWS)
        size = ALL // 2
        for start in range(0, size, TILE):
            tile = slice(part * size + start, part * size + start + TILE)
            both = weights[rows, tile] * (inverse_rows[rows, :] + across[:, tile])
            high, low = split(both)
            for i, value in enumerate((high, low, high)):
                wide[slot, :, i * size + start : i * size + start + TILE] = value
        return dot_nn(wide[slot], uj_tall[part])

    there = (1 - odd, odd)
    blocks = [b * 2 + 1 - core for b in there] + [b * 2 + core for b in there]
    take_inverse(0)
    for i, block in enumerate(blocks):
        pull_first[i] = pulls(i, block, 0)
    take_inverse(1)

    for i in range(2):
        pull_out[i] = pull_first[i] + pulls(i, blocks[i], 1)
        send(pull_out.at[i], pull_in.at[i], sib_send.at[i], sib_recv.at[i], device(dc=1))
    for i in range(2):
        pull_own[i] = pull_first[2 + i] + pulls(2 + i, blocks[2 + i], 1)

    def share(at):
        return pl.ds(pl.multiple_of(at * SHARE, SHARE), SHARE)

    for i in range(2):
        arrived(pull_in.at[i], sib_recv.at[i])
        pull_own[i] += pull_in[i]
        for dy in (2, 1, 3) if i else (2, 1, 3, 0):
            slot = dy - 1 if i else dy + 3
            send(
                pull_own.at[i, share(lax.rem(y + dy, YS))],
                shares.at[slot],
                share_send.at[slot],
                share_recv.at[slot],
                device(dy=dy, to_z=z if i else z_pair),
            )
    shares_sent = list(sent)
    sent[:] = inverse_sent
    settle()
    for slot in range(7):
        arrived(shares.at[slot], share_recv.at[slot])
    rows = pl.ds(pl.multiple_of(y * SHARE, SHARE), SHARE)
    pull = pull_own[1, share(y), :]
    for slot in range(7):
        pull = pull + shares[slot]
    unit = ui[pl.ds(pl.multiple_of(own_at + y * SHARE, SHARE), SHARE), :]
    grad_unit = INV_TEMP * (pull - 2.0 * mates[rows, :])
    along = jnp.sum(unit * grad_unit, axis=1, keepdims=True)
    grad_ref[rows, :] = (grad_unit - unit * along) / norms[rows, :]
    for dy in (2, 1, 3):
        send(
            grad_ref.at[rows],
            grad_ref.at[rows],
            grad_send.at[dy - 1],
            grad_recv.at[dy - 1],
            device(dy=dy),
        )
    sent.extend(shares_sent)
    settle()
    for dy in range(1, YS):
        from_rows = pl.ds(pl.multiple_of(lax.rem(y + YS - dy, YS) * SHARE, SHARE), SHARE)
        arrived(grad_ref.at[from_rows], grad_recv.at[dy - 1])
    settle()


def body(embeddings, partner):
    vmem = pl.BlockSpec(memory_space=pltpu.VMEM)
    hbm = pl.BlockSpec(memory_space=pltpu.HBM)
    dma = pltpu.SemaphoreType.DMA
    loss, grad = pl.pallas_call(
        kernel,
        out_shape=(
            jax.ShapeDtypeStruct((1, ROWS), F32),
            jax.ShapeDtypeStruct((ROWS, WIDTH), F32),
        ),
        in_specs=[hbm, hbm],
        out_specs=(vmem, vmem),
        scratch_shapes=[
            pltpu.VMEM((ROWS, WIDTH), F32),
            pltpu.VMEM((1, ROWS), jnp.int32),
            pltpu.VMEM((ALL, WIDTH), F32),
            pltpu.VMEM((ALL, 3 * WIDTH), BF16),
            pltpu.VMEM((ROWS, 1), F32),
            pltpu.VMEM((ROWS, WIDTH), F32),
            pltpu.VMEM((1, ROWS), F32),
            pltpu.VMEM((ALL, WIDTH), F32),
            pltpu.VMEM((ROWS, WIDTH), F32),
            pltpu.VMEM((ALL, 3 * WIDTH), BF16),
            pltpu.VMEM((2, 3 * ALL // 2, WIDTH), BF16),
            pltpu.VMEM((ALL, ALL), F32),
            pltpu.VMEM((ALL, TILE), F32),
            pltpu.VMEM((4 * YS, 4, 1, ROWS), F32),
            pltpu.VMEM((4, 1, ROWS), F32),
            pltpu.VMEM((4, 1, QUARTER), F32),
            pltpu.VMEM((ALL, TILE), F32),
            pltpu.VMEM((4, XS, 1, QUARTER), F32),
            pltpu.VMEM((1, ALL), F32),
            pltpu.VMEM((4, ROWS, 3 * ALL // 2), BF16),
            pltpu.VMEM((4, ROWS, WIDTH), F32),
            pltpu.VMEM((2, ROWS, WIDTH), F32),
            pltpu.VMEM((2, ROWS, WIDTH), F32),
            pltpu.VMEM((2, ROWS, WIDTH), F32),
            pltpu.VMEM((7, SHARE, WIDTH), F32),
            dma((2,)),
            dma((3,)),
            dma((3,)),
            dma((4,)),
            dma((4,)),
            dma((4, 3)),
            dma((4, 3)),
            dma((6,)),
            dma((6,)),
            dma((15,)),
            dma((16,)),
            dma((4, 4)),
            dma((4, 4)),
            dma((2,)),
            dma((2,)),
            dma((7,)),
            dma((7,)),
            dma((3,)),
            dma((3,)),
        ],
        compiler_params=pltpu.CompilerParams(
            collective_id=0, has_side_effects=True, vmem_limit_bytes=56254464
        ),
    )(embeddings, partner.reshape(1, ROWS))
    def write(loss_vmem, grad_vmem, loss_out, grad_out, sems):
        copies = [
            pltpu.make_async_copy(grad_vmem, grad_out, sems.at[0]),
            pltpu.make_async_copy(loss_vmem, loss_out, sems.at[1]),
        ]
        for copy in copies:
            copy.start()
        for copy in copies:
            copy.wait()

    loss, grad = pl.pallas_call(
        write,
        out_shape=(
            jax.ShapeDtypeStruct((1, ROWS), F32),
            jax.ShapeDtypeStruct((ROWS, WIDTH), F32),
        ),
        in_specs=[pl.BlockSpec(memory_space=pl.ANY)] * 2,
        out_specs=(hbm, hbm),
        scratch_shapes=[dma((2,))],
        compiler_params=pltpu.CompilerParams(vmem_limit_bytes=2**20),
    )(loss, grad)
    return loss.reshape(ROWS), grad


def solution(mesh):
    return jax.shard_map(
        body,
        mesh=mesh,
        in_specs=(P("blk", None), P("blk")),
        out_specs=(P("blk"), P("blk", None)),
        check_vma=False,
    )
```
